256 devices in a mesh: row: 8 (over z), col: 32 (over y, x, core).
Axes of the slice: x: 4, y: 4, z: 8, core: 2. Of those that a mesh axis runs over, the one named last changes fastest.
Arguments:
- prior: float32 [80, 30, 131072], P(None, None, ('row', 'col')), may hold values from -6 to 6
- ocean_mask: int32 [131072], P(('row', 'col')), may hold values from 0 to 1
- tile_order: int32 [256], replicated, may hold values from 0 to 255, each once
- obs_cell: int32 [4, 128], replicated, may hold values from 0 to 131071
- obs_stack: int32 [4, 128], replicated, may hold values from 0 to 29
- obs_values: float32 [4, 128], replicated, may hold values from -8 to 8
- window_start: int32 [4, 128], replicated, may hold values from 0 to 131071
- window_span: int32 [4, 128], replicated, may hold values from 8192 to 32768
- gain_mean: float32 [4, 128, 128], replicated, may hold values from -0.2 to 0.8
- gain_spread: float32 [4, 128, 128], replicated, may hold values from -0.2 to 0.4
Outputs:
- posterior: float32 [80, 30, 131072], P(None, None, ('row', 'col'))
The draws below stay inside these ranges and needn't reach their ends.
Inputs may be any that keep to these rules, and one draw needn't show every extreme that they name: `tile_order`: each curve tile appears once.
All inputs are finite; a program needn't handle non-finite values.
Results may differ from the reference program's by a relative error of at most 0.0001.
Values sent between devices are 32-bit elements; how exact they have to be, the bound alone decides.
No kernel may reach another device: no remote copies, remote signals or barrier semaphores. Data moves between devices by JAX's collectives and lax.ppermute only.
A program may use at most 64 MiB of HBM per device.

```python
import jax
import jax.numpy as jnp
from jax import lax

MEMBERS = 80
STACK = 30
OBS = 128
BATCHES = 4
COL_DEV = 512
NCOL = 131072
N_ROW = 8
N_COL = 32


def draw_ocean_mask(key, part):
    key_level, key_cells = jax.random.split(jax.random.fold_in(key, 3))
    tiles_count = NCOL // COL_DEV
    levels = jax.random.randint(key_level, (tiles_count, 1), 0, 5)
    patches = jax.random.randint(key_cells, (tiles_count, COL_DEV // 16), 0, 4)
    ocean = (patches < levels).astype(jnp.int32)
    return jnp.repeat(ocean, 16, axis=1).reshape(NCOL)


def factor_draw(key, lowest, highest, off_scale):
    key_diag, key_off = jax.random.split(key)
    diagonal = jnp.exp(jax.random.uniform(key_diag, (BATCHES, OBS), jnp.float32, jnp.log(lowest), jnp.log(highest)))
    off_part = off_scale * jnp.clip(jax.random.normal(key_off, (BATCHES, OBS, OBS), jnp.float32), -6.0, 6.0)
    identity = jnp.eye(OBS, dtype=jnp.float32)
    return off_part * (1.0 - identity)[None] + diagonal[:, :, None] * identity[None]


def draw_gain_mean(key, part):
    return factor_draw(jax.random.fold_in(key, 11), 0.2, 0.8, 0.02)


def draw_gain_spread(key, part):
    return factor_draw(jax.random.fold_in(key, 17), 0.1, 0.4, 0.015)


def place_ends(array, own_key, smallest, high):
    extent = array.shape
    index_at = [jax.random.randint(jax.random.fold_in(own_key, axis), (), 0, extent[axis]) for axis in range(len(extent))]
    array = array.at[tuple(index_at)].set(smallest)
    longest = extent.index(max(extent))
    index_at[longest] = (index_at[longest] + 1) % extent[longest]
    return array.at[tuple(index_at)].set(high)


def block_levels(own_key, extent, shards, low, largest):
    def one(dim, parts):
        draws = jax.random.uniform(jax.random.fold_in(jax.random.fold_in(own_key, 6), dim), (parts,), jnp.float32, low / len(shards), largest / len(shards))
        return jnp.repeat(jnp.exp(draws), extent[dim] // parts).reshape((-1,) + (1,) * (len(extent) - dim - 1))

    factor_of = one(*shards[0])
    for cut in shards[1:]:
        factor_of = factor_of * one(*cut)
    return factor_of


def bell_draw(stream_key, shape, scale, bound, cuts=(), kind=jnp.bfloat16):
    gain = block_levels(stream_key, shape, cuts, -0.22, 0.18) if cuts else 1.0
    entries = jax.random.normal(stream_key, shape, jnp.float32) * scale * gain
    return jnp.minimum(jnp.maximum(entries, -bound), bound).astype(kind)


def setup_inputs(seed: int = 0) -> dict:
    streams_of = jax.random.split(jax.random.key(seed), 11)
    return {
        "prior": bell_draw(streams_of[0], (MEMBERS, STACK, NCOL), 1.0, 6.0, ((2, 256),), jnp.float32),
        "ocean_mask": draw_ocean_mask(jax.random.fold_in(streams_of[10], 71), 0),
        "tile_order": jax.random.permutation(streams_of[2], N_ROW * N_COL).astype(jnp.int32),
        "obs_cell": place_ends(jax.random.randint(streams_of[3], (BATCHES, OBS), 0, NCOL), jax.random.fold_in(streams_of[3], 1), 0, NCOL - 1).astype(jnp.int32),
        "obs_stack": place_ends(jax.random.randint(streams_of[4], (BATCHES, OBS), 0, STACK), jax.random.fold_in(streams_of[4], 1), 0, STACK - 1).astype(jnp.int32),
        "obs_values": bell_draw(streams_of[5], (BATCHES, OBS), 1.5, 8.0, (), jnp.float32),
        "window_start": place_ends(jax.random.randint(streams_of[6], (BATCHES, OBS), 0, NCOL), jax.random.fold_in(streams_of[6], 1), 0, NCOL - 1).astype(jnp.int32),
        "window_span": place_ends(jax.random.randint(streams_of[7], (BATCHES, OBS), NCOL // 16, NCOL // 4 + 1), jax.random.fold_in(streams_of[7], 1), NCOL // 16, (NCOL // 4 + 1) - 1).astype(jnp.int32),
        "gain_mean": draw_gain_mean(jax.random.fold_in(streams_of[10], 71), 0),
        "gain_spread": draw_gain_spread(jax.random.fold_in(streams_of[10], 71), 0),
    }


HIGHEST_PRECISION = lax.Precision.HIGHEST


def regress(section, anomalies, mean_weights, spread_weights, local_weight):
    members = section.shape[0]
    centre = jnp.mean(section, axis=0)
    spread = section - centre[None]
    covariance = jnp.einsum("msc,mp->scp", spread, anomalies, precision=HIGHEST_PRECISION) / (members - 1.0)
    gain_matrix = covariance * local_weight[None]
    increment = jnp.einsum("scp,p->sc", gain_matrix, mean_weights, precision=HIGHEST_PRECISION)
    change = jnp.einsum("scp,pm->msc", gain_matrix, spread_weights, precision=HIGHEST_PRECISION)
    return centre[None] + increment[None] + spread - change


def window_weight(places, ocean_flag, starts, extents):
    inside = (places[:, None] >= starts[None, :]) & (places[:, None] < starts[None, :] + extents[None, :])
    return ocean_flag[:, None] * inside.astype(ocean_flag.dtype)


def batch_weights(priors, observed, gain_mean, gain_spread):
    centre = jnp.mean(priors, axis=0)
    anomalies = priors - centre[None]
    mean_weights = jnp.dot(gain_mean, observed - centre, precision=HIGHEST_PRECISION)
    spread_weights = jnp.dot(gain_spread, anomalies.T, precision=HIGHEST_PRECISION)
    return anomalies, mean_weights, spread_weights


def reference(prior, ocean_mask, tile_order, obs_cell, obs_stack, obs_values, window_start, window_span, gain_mean, gain_spread):
    columns_all = prior.shape[2]
    storage = jnp.arange(columns_all, dtype=jnp.int32)
    places = (tile_order[storage // COL_DEV] * COL_DEV + storage % COL_DEV).astype(jnp.int32)
    inverse = jnp.argsort(tile_order).astype(jnp.int32)
    ocean_flag = ocean_mask.astype(prior.dtype)
    ensemble = prior
    for batch_number in range(BATCHES):
        cells = obs_cell[batch_number].astype(jnp.int32)
        holder = (inverse[cells // COL_DEV] * COL_DEV + cells % COL_DEV).astype(jnp.int32)
        flattened = ensemble.reshape(MEMBERS, -1)
        spots = (obs_stack[batch_number] * columns_all + holder).astype(jnp.int32)
        priors = jnp.take(flattened, spots, axis=1)
        anomalies, mean_weights, spread_weights = batch_weights(priors, obs_values[batch_number], gain_mean[batch_number], gain_spread[batch_number])
        starts = window_start[batch_number]
        extents = window_span[batch_number]

        def advance(loop_number, current):
            offset = (loop_number * COL_DEV).astype(jnp.int32)
            section = lax.dynamic_slice_in_dim(current, offset, COL_DEV, 2)
            weight = window_weight(lax.dynamic_slice_in_dim(places, offset, COL_DEV, 0), lax.dynamic_slice_in_dim(ocean_flag, offset, COL_DEV, 0), starts, extents)
            renewed = regress(section, anomalies, mean_weights, spread_weights, weight)
            return lax.dynamic_update_slice_in_dim(current, renewed, offset, 2)

        ensemble = lax.fori_loop(0, columns_all // COL_DEV, advance, ensemble)
    return ensemble
```

```python
import functools

import jax
import jax.numpy as jnp
from jax import lax
from jax.experimental import pallas as pl
from jax.experimental.pallas import tpu as pltpu
from jax.sharding import PartitionSpec as P

ROW_COL = ("row", "col")
HIGHEST = lax.Precision.HIGHEST
F32 = jnp.float32
BF16 = jnp.bfloat16

LANES = 128
SLOTS = 9
GROUP = 4
DEPTH = 256
BIG = 1e9


def iota(shape, dim):
    return lax.broadcasted_iota(jnp.int32, shape, dim)


def as_column(row):
    size = row.shape[-1]
    eye = iota((size, size), 0) == iota((size, size), 1)
    return jnp.sum(jnp.where(eye, row, 0.0), axis=1, keepdims=True)


def dot(a, b):
    return lax.dot_general(a, b, (((1,), (0,)), ((), ())), preferred_element_type=F32)


def exact_dot(a, b, contract=0):
    return lax.dot_general(
        a, b, (((1,), (contract,)), ((), ())), precision=HIGHEST, preferred_element_type=F32
    )


def two_parts(x):
    high = x.astype(BF16)
    return high, (x - high.astype(F32)).astype(BF16)


def pick_kernel(
    members,
    columns,
    turn_s,
    tile_s,
    cells_s,
    stacks_s,
    tile_v,
    cells_v,
    start_v,
    span_v,
    ocean_v,
    prior,
    packed,
    index_v,
    bounds_s,
    counts_s,
    owned_s,
    held,
    sems,
):
    batches, obs = cells_v.shape
    total = batches * obs
    devices = tile_s.shape[0]
    device = lax.axis_index("row") * lax.axis_size("col") + lax.axis_index("col")
    mine = tile_s[device]
    first = turn_s[0] * SLOTS

    def scan(step, count):
        for inner in range(16):
            n = step * 16 + inner
            owned_s[count] = n
            count = count + (cells_s[n] // columns == mine).astype(jnp.int32)
        return count

    count = lax.fori_loop(0, total // 16, scan, jnp.int32(0))
    here = jnp.clip(count - first, 0, SLOTS)

    def fetch(k):
        n = owned_s[first + k]
        column = cells_s[n] % columns
        lane = pl.multiple_of(column // LANES * LANES, LANES)
        return pltpu.make_async_copy(
            prior.at[:, stacks_s[n], pl.ds(lane, LANES)], held.at[k], sems.at[k]
        )

    @pl.loop(0, here)
    def _(k):
        fetch(k).start()

    cells = cells_v[...]
    tiles = (cells // columns).astype(F32)
    tile_columns = [as_column(tiles[b : b + 1]) for b in range(batches)]
    order = tile_v[...].astype(F32)
    order_columns = [as_column(order[h : h + 1]) for h in range(devices // LANES)]
    above = iota((obs, obs), 0) < iota((obs, obs), 1)
    ids = iota((obs, obs), 0).astype(F32)
    ranks = []
    for b in range(batches):
        same = [tile_columns[a] == tiles[b : b + 1] for a in range(b + 1)]
        same[b] = same[b] & above
        rank = sum(jnp.sum(jnp.where(s, 1.0, 0.0), axis=0, keepdims=True) for s in same)
        owner = sum(
            jnp.sum(
                jnp.where(order_columns[h] == tiles[b : b + 1], ids + float(h * LANES), 0.0),
                axis=0,
                keepdims=True,
            )
            for h in range(devices // LANES)
        )
        index_v[b : b + 1, :] = (rank * float(devices) + owner).astype(jnp.int32)
        ranks.append(rank)
    highest = jnp.max(jnp.concatenate(ranks, axis=0)).astype(jnp.int32)
    counts_s[1] = highest // SLOTS + 1

    begin = start_v[...] - mine * columns
    edges = jnp.concatenate([begin, begin + span_v[...]], axis=0).astype(F32)
    edges = jnp.where(edges < float(columns), edges, BIG)
    bounds_s[0] = 0

    def next_edge(state):
        at, found = state
        later = jnp.min(jnp.where(edges > at.astype(F32), edges, BIG))
        at = jnp.minimum(later, float(columns)).astype(jnp.int32)
        bounds_s[found + 1] = at
        return at, found + 1

    _, found = lax.while_loop(lambda s: s[0] < columns, next_edge, (jnp.int32(0), jnp.int32(0)))
    counts_s[0] = found
    for k in range(GROUP):
        bounds_s[found + 1 + k] = columns

    lane_of = iota((members, LANES), 1)
    places = iota((columns // LANES, LANES), 0) * LANES + iota((columns // LANES, LANES), 1)
    ocean = ocean_v[...].astype(F32)

    def gather(k, state):
        values, flags = state
        fetch(k).wait()
        column = cells_s[owned_s[first + k]] % columns
        one = jnp.sum(
            jnp.where(lane_of == column % LANES, held[k], 0.0), axis=1, keepdims=True
        )
        flag = jnp.sum(jnp.where(places == column, ocean, 0.0))
        values = jnp.where(lane_of == k, one, values)
        flags = jnp.where(iota((8, LANES), 1) == k, flag, flags)
        return values, flags

    values, flags = lax.fori_loop(
        0, here, gather, (jnp.zeros((members, LANES), F32), jnp.zeros((8, LANES), F32))
    )
    spare = jnp.zeros((LANES - members - 8, LANES), F32)
    rows = jnp.concatenate([values, flags, spare], axis=0).T
    width = members + 1
    lanes = iota((1, LANES), 1)
    pieces = [jnp.zeros((1, LANES), F32) for _ in range(packed.shape[1] // LANES)]
    for k in range(SLOTS):
        chunk, shift = divmod(k * width, LANES)
        row = rows[k : k + 1]
        row = jnp.where(lanes < width, row, 0.0)
        if shift:
            row = pltpu.roll(row, shift, 1)
        pieces[chunk] = pieces[chunk] + jnp.where(lanes >= shift, row, 0.0)
        if shift + width > LANES:
            pieces[chunk + 1] = pieces[chunk + 1] + jnp.where(lanes < shift, row, 0.0)
    packed[...] = jnp.concatenate(pieces, axis=1)


def place_kernel(members, turn_s, index_s, before, arrived, out, rows):
    devices = arrived.shape[0]
    width = members + 1
    lanes = iota((devices, LANES), 1)
    for k in range(SLOTS):
        chunk, shift = divmod(k * width, LANES)
        part = arrived[:, chunk * LANES : (chunk + 1) * LANES]
        if shift:
            part = pltpu.roll(part, LANES - shift, 1)
        if shift + width > LANES:
            after = arrived[:, (chunk + 1) * LANES : (chunk + 2) * LANES]
            after = pltpu.roll(after, LANES - shift, 1)
            part = jnp.where(lanes < LANES - shift, part, after)
        rows[k * devices : (k + 1) * devices, :] = jnp.where(lanes < width, part, 0.0)
    base = turn_s[0] * (SLOTS * devices)
    last = SLOTS * devices - 1

    @pl.loop(0, out.shape[0] // 16)
    def _(step):
        for inner in range(16):
            n = step * 16 + inner
            at = index_s[n] - base
            held_now = (at >= 0) & (at <= last)
            row = rows[pl.ds(jnp.clip(at, 0, last), 1), :]
            out[pl.ds(n, 1), :] = jnp.where(held_now, row, before[pl.ds(n, 1), :])


def sweep_kernel(
    members,
    bounds_s,
    counts_s,
    tile_s,
    obs_v,
    cells_v,
    start_v,
    span_v,
    gain_mean,
    gain_spread,
    ocean_v,
    priors,
    prior,
    out,
    state,
    parts,
    values,
    weights_f,
    weights_p,
    anoms_p,
    maps_f,
    maps_p,
    load_sems,
    store_sems,
):
    stack, columns = prior.shape[1], prior.shape[2]
    batches, obs = cells_v.shape
    device = lax.axis_index("row") * lax.axis_size("col") + lax.axis_index("col")
    base = tile_s[device] * columns

    @pl.loop(0, stack)
    def _(v):
        pltpu.make_async_copy(prior.at[:, v, :], state.at[v], load_sems.at[v]).start()

    values[...] = priors[...]
    lanes = iota((1, LANES), 1)
    member = lanes < members

    def centred(block):
        mean = jnp.sum(jnp.where(member, block, 0.0), axis=1, keepdims=True) * (1.0 / members)
        return mean, jnp.where(member, block - mean, 0.0)

    for b in range(batches):
        mean, anomalies = centred(values[b * obs : (b + 1) * obs, :])
        innovation = as_column(obs_v[b : b + 1, :]) - mean
        gains = jnp.concatenate([gain_mean[b], -gain_spread[b]], axis=1)
        against = jnp.concatenate(
            [jnp.broadcast_to(innovation, (obs, LANES)), anomalies], axis=0
        )
        weights = jnp.where(member, exact_dot(gains, against), 0.0)
        scaled = anomalies * (1.0 / (members - 1.0))
        if b + 1 < batches:
            later = values[(b + 1) * obs :, :]
            _, spread = centred(later)
            gain = exact_dot(spread, scaled, 1)
            cells = jnp.concatenate(
                [
                    as_column(cells_v[a : a + 1, :].astype(F32))
                    for a in range(b + 1, batches)
                ],
                axis=0,
            )
            begin = start_v[b : b + 1, :].astype(F32)
            end = begin + span_v[b : b + 1, :].astype(F32)
            wet = later[:, members : members + 1]
            gain = jnp.where((cells >= begin) & (cells < end), gain * wet, 0.0)
            values[(b + 1) * obs :, :] = later + exact_dot(gain, weights)
        across = weights.T
        weights_f[b] = across[:members]
        high, low = two_parts(across[:members])
        weights_p[b] = jnp.concatenate([high, low, high, jnp.zeros((DEPTH - 3 * members, obs), BF16)], axis=0)
        wide = jnp.concatenate([-scaled, jnp.zeros_like(scaled)], axis=1)
        wide = wide + pltpu.roll(wide, members, 1) + pltpu.roll(wide, 2 * members, 1)
        high, low = two_parts(wide)
        anoms_p[b] = jnp.concatenate([high, high, low], axis=0)

    @pl.loop(0, stack)
    def _(v):
        pltpu.make_async_copy(prior.at[:, v, :], state.at[v], load_sems.at[v]).wait()
        block = state[v]
        spread = block - jnp.sum(block, axis=0, keepdims=True) * (1.0 / members)
        high, low = two_parts(spread)
        parts[v, 0:members, :] = high
        parts[v, members : 2 * members, :] = low
        parts[v, 2 * members : 3 * members, :] = high
        parts[v, 3 * members :, :] = jnp.zeros((DEPTH - 3 * members, columns), BF16)

    segments = counts_s[0]
    wide_lane = iota((GROUP * members, DEPTH), 1)

    @pl.loop(0, pl.cdiv(segments, GROUP))
    def _(group):
        first = group * GROUP
        bounds = [bounds_s[first + k] for k in range(GROUP + 1)]
        for b in reversed(range(batches)):
            begin = start_v[b : b + 1, :]
            end = begin + span_v[b : b + 1, :]
            if b < batches - 1:
                grown = dot(maps_p[...], weights_p[b])
            pieces = []
            for k in range(GROUP):
                at = base + bounds[k]
                piece = weights_f[b]
                if b < batches - 1:
                    piece = piece + grown[k * members : (k + 1) * members]
                pieces.append(jnp.where((begin <= at) & (at < end), piece, 0.0))
            high, low = two_parts(jnp.concatenate(pieces, axis=0))
            maps = dot(jnp.concatenate([high, low, high], axis=1), anoms_p[b])
            maps = (maps_f[...] if b < batches - 1 else 0.0) - maps
            maps_f[...] = maps
            rest = maps - maps.astype(BF16).astype(F32)
            maps_p[...] = jnp.where(wide_lane < 2 * members, maps, rest).astype(BF16)

        half = columns // 2
        for c in range(0, columns, half):
            place = c + iota((1, half), 1)
            wet = ocean_v[0:1, c : c + half] > 0
            inside = [wet & (place >= bounds[k]) & (place < bounds[k + 1]) for k in range(GROUP)]

            @pl.when((bounds[0] < c + half) & (bounds[GROUP] > c))
            def _():
                @pl.loop(0, stack)
                def _(v):
                    change = dot(maps_p[...], parts[v, :, c : c + half])
                    moved = jnp.zeros((members, half), F32)
                    for k in range(GROUP):
                        moved = jnp.where(
                            inside[k], change[k * members : (k + 1) * members], moved
                        )
                    state[v, :, c : c + half] = state[v, :, c : c + half] + moved

    @pl.loop(0, stack)
    def _(v):
        pltpu.make_async_copy(state.at[v], out.at[:, v, :], store_sems.at[v]).start()

    @pl.loop(0, stack)
    def _(v):
        pltpu.make_async_copy(state.at[v], out.at[:, v, :], store_sems.at[v]).wait()


def per_device(
    prior,
    ocean_mask,
    tile_order,
    obs_cell,
    obs_stack,
    obs_values,
    window_start,
    window_span,
    gain_mean,
    gain_spread,
):
    members, stack, columns = prior.shape
    batches, obs = obs_cell.shape
    total = batches * obs
    devices = tile_order.shape[0]
    wide = -(-SLOTS * (members + 1) // LANES) * LANES
    smem = pl.BlockSpec(memory_space=pltpu.SMEM)
    vmem = pl.BlockSpec(memory_space=pltpu.VMEM)
    hbm = pl.BlockSpec(memory_space=pl.ANY)
    cells_flat = obs_cell.reshape(-1)
    stacks_flat = obs_stack.reshape(-1)
    tiles_2d = tile_order.reshape(-1, LANES)
    limit = 48 * 1024 * 1024

    def pick(turn):
        return pl.pallas_call(
            functools.partial(pick_kernel, members, columns),
            out_shape=(
                jax.ShapeDtypeStruct((1, wide), F32),
                jax.ShapeDtypeStruct((batches, obs), jnp.int32),
                jax.ShapeDtypeStruct((columns + 1 + GROUP,), jnp.int32),
                jax.ShapeDtypeStruct((2,), jnp.int32),
            ),
            in_specs=[smem] * 4 + [vmem] * 5 + [hbm],
            out_specs=(vmem, vmem, smem, smem),
            scratch_shapes=[
                pltpu.SMEM((total + 1 + SLOTS,), jnp.int32),
                pltpu.VMEM((SLOTS, members, LANES), F32),
                pltpu.SemaphoreType.DMA((SLOTS,)),
            ],
            compiler_params=pltpu.CompilerParams(vmem_limit_bytes=limit),
        )(
            turn,
            tile_order,
            cells_flat,
            stacks_flat,
            tiles_2d,
            obs_cell,
            window_start,
            window_span,
            ocean_mask.reshape(-1, LANES),
            prior,
        )

    def place(turn, index, before, packed):
        sent = jnp.broadcast_to(packed[None], (devices, 1, wide))
        arrived = lax.all_to_all(sent, ROW_COL, 0, 0, tiled=True).reshape(devices, wide)
        return pl.pallas_call(
            functools.partial(place_kernel, members),
            out_shape=jax.ShapeDtypeStruct((total, LANES), F32),
            in_specs=[smem, smem, vmem, vmem],
            out_specs=vmem,
            scratch_shapes=[pltpu.VMEM((SLOTS * devices, LANES), F32)],
            compiler_params=pltpu.CompilerParams(vmem_limit_bytes=limit),
        )(turn, index, before, arrived)

    turn = jnp.zeros((1,), jnp.int32)
    packed, index, bounds, counts = pick(turn)
    index = index.reshape(-1)
    values = place(turn, index, jnp.zeros((total, LANES), F32), packed)

    def again(state):
        turn, before = state
        return turn + 1, place(turn, index, before, pick(turn)[0])

    _, values = lax.while_loop(lambda s: s[0][0] < counts[1], again, (turn + 1, values))

    return pl.pallas_call(
        functools.partial(sweep_kernel, members),
        out_shape=jax.ShapeDtypeStruct(prior.shape, F32),
        in_specs=[smem] * 3 + [vmem] * 8 + [hbm],
        out_specs=hbm,
        scratch_shapes=[
            pltpu.VMEM((stack, members, columns), F32),
            pltpu.VMEM((stack, DEPTH, columns), BF16),
            pltpu.VMEM((total, LANES), F32),
            pltpu.VMEM((batches, members, obs), F32),
            pltpu.VMEM((batches, DEPTH, obs), BF16),
            pltpu.VMEM((batches, 3 * obs, DEPTH), BF16),
            pltpu.VMEM((GROUP * members, DEPTH), F32),
            pltpu.VMEM((GROUP * members, DEPTH), BF16),
            pltpu.SemaphoreType.DMA((stack,)),
            pltpu.SemaphoreType.DMA((stack,)),
        ],
        compiler_params=pltpu.CompilerParams(vmem_limit_bytes=limit),
    )(
        bounds,
        counts,
        tile_order,
        obs_values,
        obs_cell,
        window_start,
        window_span,
        gain_mean,
        gain_spread,
        ocean_mask.reshape(1, -1),
        values,
        prior,
    )


def solution(mesh):
    in_specs = (P(None, None, ROW_COL), P(ROW_COL), P(), P(), P(), P(), P(), P(), P(), P())
    return jax.shard_map(
        per_device, mesh=mesh, in_specs=in_specs, out_specs=P(None, None, ROW_COL), check_vma=False
    )
```

```python
import functools

import jax
import jax.numpy as jnp
from jax import lax
from jax.experimental import pallas as pl
from jax.experimental.pallas import tpu as pltpu
from jax.sharding import PartitionSpec as P

ROW_COL = ("row", "col")
HIGHEST = lax.Precision.HIGHEST
F32 = jnp.float32
BF16 = jnp.bfloat16

LANES = 128
SLOTS = 9
GROUP = 4
DEPTH = 256
CHUNK = 128
UNROLL = 30
BIG = 1e9


def iota(shape, dim):
    return lax.broadcasted_iota(jnp.int32, shape, dim)


def as_column(row):
    size = row.shape[-1]
    eye = iota((size, size), 0) == iota((size, size), 1)
    return jnp.sum(jnp.where(eye, row, 0.0), axis=1, keepdims=True)


def dot(a, b):
    return lax.dot_general(a, b, (((1,), (0,)), ((), ())), preferred_element_type=F32)


def exact_dot(a, b, contract=0):
    return lax.dot_general(
        a, b, (((1,), (contract,)), ((), ())), precision=HIGHEST, preferred_element_type=F32
    )


def two_parts(x):
    high = x.astype(BF16)
    return high, (x - high.astype(F32)).astype(BF16)


def my_device():
    return lax.axis_index("row") * lax.axis_size("col") + lax.axis_index("col")


def pick_kernel(
    columns, turn_s, tile_s, cells_s, stacks_s, cells_v, ocean_v, prior, packed, owned_s, held, sems
):
    batches, obs = cells_v.shape
    members = prior.shape[1]
    mine = tile_s[my_device()]
    first = turn_s[0] * SLOTS
    numbers = (iota((batches, obs), 0) * obs + iota((batches, obs), 1)).astype(F32)
    numbers = jnp.where(cells_v[...] // columns == mine, numbers, BIG)

    def fetch(k):
        n = owned_s[k]
        lane = pl.multiple_of(cells_s[n] % columns // LANES * LANES, LANES)
        return pltpu.make_async_copy(
            prior.at[stacks_s[n], :, pl.ds(lane, LANES)], held.at[k], sems.at[k]
        )

    def after(n):
        return jnp.min(jnp.where(numbers > n, numbers, BIG))

    def find(state):
        n, rank = state

        @pl.when(rank >= first)
        def _():
            owned_s[rank - first] = n.astype(jnp.int32)
            fetch(rank - first).start()

        return after(n), rank + 1

    _, found = lax.while_loop(
        lambda s: (s[0] < BIG) & (s[1] < first + SLOTS), find, (after(-1.0), jnp.int32(0))
    )
    here = jnp.maximum(found - first, 0)

    lane_of = iota((members, LANES), 1)
    places = iota((columns // LANES, LANES), 0) * LANES + iota((columns // LANES, LANES), 1)
    ocean = ocean_v[...].astype(F32)

    def gather(k, state):
        values, flags = state
        fetch(k).wait()
        column = cells_s[owned_s[k]] % columns
        one = jnp.sum(
            jnp.where(lane_of == column % LANES, held[k], 0.0), axis=1, keepdims=True
        )
        flag = jnp.sum(jnp.where(places == column, ocean, 0.0))
        values = jnp.where(lane_of == k, one, values)
        flags = jnp.where(iota((8, LANES), 1) == k, flag, flags)
        return values, flags

    values, flags = lax.fori_loop(
        0, here, gather, (jnp.zeros((members, LANES), F32), jnp.zeros((8, LANES), F32))
    )
    spare = jnp.zeros((LANES - members - 8, LANES), F32)
    rows = jnp.concatenate([values, flags, spare], axis=0).T
    width = members + 1
    lanes = iota((1, LANES), 1)
    pieces = [jnp.zeros((1, LANES), F32) for _ in range(packed.shape[1] // LANES)]
    for k in range(SLOTS):
        chunk, shift = divmod(k * width, LANES)
        row = rows[k : k + 1]
        row = jnp.where(lanes < width, row, 0.0)
        if shift:
            row = pltpu.roll(row, shift, 1)
        pieces[chunk] = pieces[chunk] + jnp.where(lanes >= shift, row, 0.0)
        if shift + width > LANES:
            pieces[chunk + 1] = pieces[chunk + 1] + jnp.where(lanes < shift, row, 0.0)
    packed[...] = jnp.concatenate(pieces, axis=1)


def index_kernel(
    columns, tile_s, tile_v, cells_v, start_v, span_v, index_v, bounds_s, segments_s, rounds_s
):
    batches, obs = cells_v.shape
    devices = tile_s.shape[0]
    mine = tile_s[my_device()]

    cells = cells_v[...]
    tiles = (cells // columns).astype(F32)
    tile_columns = [as_column(tiles[b : b + 1]) for b in range(batches)]
    order = tile_v[...].astype(F32)
    order_columns = [as_column(order[h : h + 1]) for h in range(devices // LANES)]
    above = iota((obs, obs), 0) < iota((obs, obs), 1)
    ids = iota((obs, obs), 0).astype(F32)
    ranks = []
    for b in range(batches):
        same = [tile_columns[a] == tiles[b : b + 1] for a in range(b + 1)]
        same[b] = same[b] & above
        rank = sum(jnp.sum(jnp.where(s, 1.0, 0.0), axis=0, keepdims=True) for s in same)
        owner = sum(
            jnp.sum(
                jnp.where(order_columns[h] == tiles[b : b + 1], ids + float(h * LANES), 0.0),
                axis=0,
                keepdims=True,
            )
            for h in range(devices // LANES)
        )
        index_v[b : b + 1, :] = (rank * float(devices) + owner).astype(jnp.int32)
        ranks.append(rank)
    highest = jnp.max(jnp.concatenate(ranks, axis=0)).astype(jnp.int32)
    rounds_s[0] = highest // SLOTS + 1

    begin = start_v[...] - mine * columns
    edges = jnp.concatenate([begin, begin + span_v[...]], axis=0).astype(F32)
    edges = jnp.where(edges < float(columns), edges, BIG)
    bounds_s[0] = 0

    def next_edge(state):
        at, found = state
        later = jnp.min(jnp.where(edges > at.astype(F32), edges, BIG))
        at = jnp.minimum(later, float(columns)).astype(jnp.int32)
        bounds_s[found + 1] = at
        return at, found + 1

    _, found = lax.while_loop(lambda s: s[0] < columns, next_edge, (jnp.int32(0), jnp.int32(0)))
    segments_s[0] = found
    for k in range(GROUP):
        bounds_s[found + 1 + k] = columns


def split_kernel(prior, parts):
    members, columns = prior.shape[1:]
    block = prior[0]
    spread = block - jnp.sum(block, axis=0, keepdims=True) * (1.0 / members)
    high, low = two_parts(spread)
    parts[0, 0:members, :] = high
    parts[0, members : 2 * members, :] = low
    parts[0, 2 * members : 3 * members, :] = high
    parts[0, 3 * members :, :] = jnp.zeros((DEPTH - 3 * members, columns), BF16)


def place_kernel(members, turn_s, index_s, arrived, *refs):
    *before, out, rows = refs
    devices = arrived.shape[0]
    width = members + 1
    lanes = iota((devices, LANES), 1)
    for k in range(SLOTS):
        chunk, shift = divmod(k * width, LANES)
        part = arrived[:, chunk * LANES : (chunk + 1) * LANES]
        if shift:
            part = pltpu.roll(part, LANES - shift, 1)
        if shift + width > LANES:
            after = arrived[:, (chunk + 1) * LANES : (chunk + 2) * LANES]
            after = pltpu.roll(after, LANES - shift, 1)
            part = jnp.where(lanes < LANES - shift, part, after)
        rows[k * devices : (k + 1) * devices, :] = jnp.where(lanes < width, part, 0.0)
    base = turn_s[0] * (SLOTS * devices)
    last = SLOTS * devices - 1

    @pl.loop(0, out.shape[0] // 16)
    def _(step):
        for inner in range(16):
            n = step * 16 + inner
            at = index_s[n] - base
            row = rows[pl.ds(jnp.clip(at, 0, last), 1), :]
            if before:
                row = jnp.where((at >= 0) & (at <= last), row, before[0][pl.ds(n, 1), :])
            out[pl.ds(n, 1), :] = row


def sweep_kernel(
    members,
    bounds_s,
    segments_s,
    tile_s,
    obs_v,
    cells_v,
    start_v,
    span_v,
    gain_mean,
    gain_spread,
    ocean_v,
    priors,
    split,
    prior,
    out,
    state,
    parts,
    values,
    weights_f,
    weights_p,
    anoms_p,
    maps_f,
    maps_p,
    sems,
):
    stack, _, columns = prior.shape
    batches, obs = cells_v.shape
    base = tile_s[my_device()] * columns
    loads = [
        pltpu.make_async_copy(split, parts, sems.at[0]),
        pltpu.make_async_copy(prior, state, sems.at[1]),
    ]
    for load in loads:
        load.start()

    values[...] = priors[...]
    lanes = iota((1, LANES), 1)
    member = lanes < members

    def centred(block):
        mean = jnp.sum(jnp.where(member, block, 0.0), axis=1, keepdims=True) * (1.0 / members)
        return mean, jnp.where(member, block - mean, 0.0)

    for b in range(batches):
        mean, anomalies = centred(values[b * obs : (b + 1) * obs, :])
        innovation = as_column(obs_v[b : b + 1, :]) - mean
        gains = jnp.concatenate([gain_mean[b], -gain_spread[b]], axis=1)
        against = jnp.concatenate(
            [jnp.broadcast_to(innovation, (obs, LANES)), anomalies], axis=0
        )
        weights = jnp.where(member, exact_dot(gains, against), 0.0)
        scaled = anomalies * (1.0 / (members - 1.0))
        if b + 1 < batches:
            later = values[(b + 1) * obs :, :]
            _, spread = centred(later)
            gain = exact_dot(spread, scaled, 1)
            cells = jnp.concatenate(
                [
                    as_column(cells_v[a : a + 1, :].astype(F32))
                    for a in range(b + 1, batches)
                ],
                axis=0,
            )
            begin = start_v[b : b + 1, :].astype(F32)
            end = begin + span_v[b : b + 1, :].astype(F32)
            wet = later[:, members : members + 1]
            gain = jnp.where((cells >= begin) & (cells < end), gain * wet, 0.0)
            values[(b + 1) * obs :, :] = later + exact_dot(gain, weights)
        across = weights.T
        weights_f[b] = across[:members]
        high, low = two_parts(across[:members])
        weights_p[b] = jnp.concatenate([high, low, high, jnp.zeros((DEPTH - 3 * members, obs), BF16)], axis=0)
        wide = jnp.concatenate([-scaled, jnp.zeros_like(scaled)], axis=1)
        wide = wide + pltpu.roll(wide, members, 1) + pltpu.roll(wide, 2 * members, 1)
        high, low = two_parts(wide)
        anoms_p[b] = jnp.concatenate([high, high, low], axis=0)

    for load in loads:
        load.wait()
    segments = segments_s[0]

    def store(c):
        where = pl.ds(pl.multiple_of(c * CHUNK, CHUNK), CHUNK)
        return pltpu.make_async_copy(state.at[:, :, where], out.at[:, :, where], sems.at[2 + c])

    wide_lane = iota((GROUP * members, DEPTH), 1)

    @pl.loop(0, pl.cdiv(segments, GROUP))
    def _(group):
        first = group * GROUP
        bounds = [bounds_s[first + k] for k in range(GROUP + 1)]
        for b in reversed(range(batches)):
            begin = start_v[b : b + 1, :]
            end = begin + span_v[b : b + 1, :]
            if b < batches - 1:
                grown = dot(maps_p[...], weights_p[b])
            pieces = []
            for k in range(GROUP):
                at = base + bounds[k]
                piece = weights_f[b]
                if b < batches - 1:
                    piece = piece + grown[k * members : (k + 1) * members]
                pieces.append(jnp.where((begin <= at) & (at < end), piece, 0.0))
            high, low = two_parts(jnp.concatenate(pieces, axis=0))
            maps = dot(jnp.concatenate([high, low, high], axis=1), anoms_p[b])
            maps = (maps_f[...] if b < batches - 1 else 0.0) - maps
            maps_f[...] = maps
            rest = maps - maps.astype(BF16).astype(F32)
            maps_p[...] = jnp.where(wide_lane < 2 * members, maps, rest).astype(BF16)

        @pl.loop(0, jnp.minimum(segments - first, GROUP))
        def _(k):
            low, high = bounds_s[first + k], bounds_s[first + k + 1]

            @pl.loop(low // CHUNK, pl.cdiv(high, CHUNK))
            def _(c):
                at = pl.multiple_of(c * CHUNK, CHUNK)
                place = at + iota((1, CHUNK), 1)
                inside = (place >= low) & (place < high)
                inside = inside & (ocean_v[0:1, pl.ds(at, CHUNK)] > 0)
                own_map = maps_p[pl.ds(pl.multiple_of(k * members, 16), members), :]

                @pl.loop(0, stack, unroll=UNROLL)
                def _(v):
                    change = dot(own_map, parts[v, :, pl.ds(at, CHUNK)])
                    before = state[v, :, pl.ds(at, CHUNK)]
                    state[v, :, pl.ds(at, CHUNK)] = jnp.where(inside, before + change, before)

                @pl.when(high >= at + CHUNK)
                def _():
                    store(c).start()

    for c in range(columns // CHUNK):
        store(c).wait()


def per_device(
    prior,
    ocean_mask,
    tile_order,
    obs_cell,
    obs_stack,
    obs_values,
    window_start,
    window_span,
    gain_mean,
    gain_spread,
):
    members, stack, columns = prior.shape
    batches, obs = obs_cell.shape
    total = batches * obs
    devices = tile_order.shape[0]
    wide = -(-SLOTS * (members + 1) // LANES) * LANES
    smem = pl.BlockSpec(memory_space=pltpu.SMEM)
    vmem = pl.BlockSpec(memory_space=pltpu.VMEM)
    hbm = pl.BlockSpec(memory_space=pl.ANY)
    cells_flat = obs_cell.reshape(-1)
    stacks_flat = obs_stack.reshape(-1)
    tiles_2d = tile_order.reshape(-1, LANES)
    limit = 32 * 1024 * 1024

    params = pltpu.CompilerParams(vmem_limit_bytes=limit)
    by_stack = prior.transpose(1, 0, 2)

    def pick(turn):
        return pl.pallas_call(
            functools.partial(pick_kernel, columns),
            out_shape=jax.ShapeDtypeStruct((1, wide), F32),
            in_specs=[smem] * 4 + [vmem] * 2 + [hbm],
            out_specs=vmem,
            scratch_shapes=[
                pltpu.SMEM((SLOTS,), jnp.int32),
                pltpu.VMEM((SLOTS, members, LANES), F32),
                pltpu.SemaphoreType.DMA((SLOTS,)),
            ],
            compiler_params=params,
            name="pick",
        )(
            turn,
            tile_order,
            cells_flat,
            stacks_flat,
            obs_cell,
            ocean_mask.reshape(-1, LANES),
            by_stack,
        )

    def place(turn, index, packed, *before):
        sent = jnp.broadcast_to(packed[None], (devices, 1, wide))
        arrived = lax.all_to_all(sent, ROW_COL, 0, 0, tiled=True).reshape(devices, wide)
        return pl.pallas_call(
            functools.partial(place_kernel, members),
            out_shape=jax.ShapeDtypeStruct((total, LANES), F32),
            in_specs=[smem, smem, vmem] + [vmem] * len(before),
            out_specs=vmem,
            scratch_shapes=[pltpu.VMEM((SLOTS * devices, LANES), F32)],
            compiler_params=params,
            name="place",
        )(turn, index, arrived, *before)

    turn = jnp.zeros((1,), jnp.int32)
    packed = pick(turn)
    index, bounds, segments, rounds = pl.pallas_call(
        functools.partial(index_kernel, columns),
        out_shape=(
            jax.ShapeDtypeStruct((batches, obs), jnp.int32),
            jax.ShapeDtypeStruct((columns + 1 + GROUP,), jnp.int32),
            jax.ShapeDtypeStruct((1,), jnp.int32),
            jax.ShapeDtypeStruct((1,), jnp.int32),
        ),
        in_specs=[smem] + [vmem] * 4,
        out_specs=(vmem, smem, smem, smem),
        compiler_params=params,
        name="index",
    )(tile_order, tiles_2d, obs_cell, window_start, window_span)
    parts = pl.pallas_call(
        split_kernel,
        out_shape=jax.ShapeDtypeStruct((stack, DEPTH, columns), BF16),
        grid=(stack,),
        in_specs=[pl.BlockSpec((1, members, columns), lambda v: (v, 0, 0))],
        out_specs=pl.BlockSpec((1, DEPTH, columns), lambda v: (v, 0, 0)),
        compiler_params=params,
        name="split",
    )(by_stack)
    index = index.reshape(-1)
    values = place(turn, index, packed)

    def again(state):
        turn, before = state
        return turn + 1, place(turn, index, pick(turn), before)

    _, values = lax.while_loop(lambda s: (s[0] < rounds)[0], again, (turn + 1, values))

    posterior = pl.pallas_call(
        functools.partial(sweep_kernel, members),
        out_shape=jax.ShapeDtypeStruct((stack, members, columns), F32),
        in_specs=[smem] * 3 + [vmem] * 8 + [hbm] * 2,
        out_specs=hbm,
        scratch_shapes=[
            pltpu.VMEM((stack, members, columns), F32),
            pltpu.VMEM((stack, DEPTH, columns), BF16),
            pltpu.VMEM((total, LANES), F32),
            pltpu.VMEM((batches, members, obs), F32),
            pltpu.VMEM((batches, DEPTH, obs), BF16),
            pltpu.VMEM((batches, 3 * obs, DEPTH), BF16),
            pltpu.VMEM((GROUP * members, DEPTH), F32),
            pltpu.VMEM((GROUP * members, DEPTH), BF16),
            pltpu.SemaphoreType.DMA((2 + columns // CHUNK,)),
        ],
        compiler_params=params,
        name="sweep",
    )(
        bounds,
        segments,
        tile_order,
        obs_values,
        obs_cell,
        window_start,
        window_span,
        gain_mean,
        gain_spread,
        ocean_mask.reshape(1, -1),
        values,
        parts,
        by_stack,
    )
    return posterior.transpose(1, 0, 2)


def solution(mesh):
    in_specs = (P(None, None, ROW_COL), P(ROW_COL), P(), P(), P(), P(), P(), P(), P(), P())
    return jax.shard_map(
        per_device, mesh=mesh, in_specs=in_specs, out_specs=P(None, None, ROW_COL), check_vma=False
    )
```

```python
import functools

import jax
import jax.numpy as jnp
from jax import lax
from jax.experimental import pallas as pl
from jax.experimental.pallas import tpu as pltpu
from jax.sharding import PartitionSpec as P

ROW_COL = ("row", "col")
HIGHEST = lax.Precision.HIGHEST
F32 = jnp.float32
BF16 = jnp.bfloat16

LANES = 128
SLOTS = 9
GROUP = 4
DEPTH = 256
CHUNK = 128
UNROLL = 30
BIG = 1e9


def iota(shape, dim):
    return lax.broadcasted_iota(jnp.int32, shape, dim)


def as_column(row):
    size = row.shape[-1]
    eye = iota((size, size), 0) == iota((size, size), 1)
    return jnp.sum(jnp.where(eye, row, 0.0), axis=1, keepdims=True)


def dot(a, b):
    return lax.dot_general(a, b, (((1,), (0,)), ((), ())), preferred_element_type=F32)


def exact_dot(a, b, contract=0):
    return lax.dot_general(
        a, b, (((1,), (contract,)), ((), ())), precision=HIGHEST, preferred_element_type=F32
    )


def two_parts(x):
    high = x.astype(BF16)
    return high, (x - high.astype(F32)).astype(BF16)


def my_device():
    return lax.axis_index("row") * lax.axis_size("col") + lax.axis_index("col")


def pick_kernel(
    columns, turn_s, tile_s, cells_s, stacks_s, cells_v, ocean_v, prior, packed, owned_s, held, sems
):
    batches, obs = cells_v.shape
    members = prior.shape[1]
    mine = tile_s[my_device()]
    first = turn_s[0] * SLOTS
    numbers = (iota((batches, obs), 0) * obs + iota((batches, obs), 1)).astype(F32)
    numbers = jnp.where(cells_v[...] // columns == mine, numbers, BIG)

    def fetch(k):
        n = owned_s[k]
        lane = pl.multiple_of(cells_s[n] % columns // LANES * LANES, LANES)
        return pltpu.make_async_copy(
            prior.at[stacks_s[n], :, pl.ds(lane, LANES)], held.at[k], sems.at[k]
        )

    def after(n):
        return jnp.min(jnp.where(numbers > n, numbers, BIG))

    def find(state):
        n, rank = state

        @pl.when(rank >= first)
        def _():
            owned_s[rank - first] = n.astype(jnp.int32)
            fetch(rank - first).start()

        return after(n), rank + 1

    _, found = lax.while_loop(
        lambda s: (s[0] < BIG) & (s[1] < first + SLOTS), find, (after(-1.0), jnp.int32(0))
    )
    here = jnp.maximum(found - first, 0)

    lane_of = iota((members, LANES), 1)
    places = iota((columns // LANES, LANES), 0) * LANES + iota((columns // LANES, LANES), 1)
    ocean = ocean_v[...].astype(F32)

    def gather(k, state):
        values, flags = state
        fetch(k).wait()
        column = cells_s[owned_s[k]] % columns
        one = jnp.sum(
            jnp.where(lane_of == column % LANES, held[k], 0.0), axis=1, keepdims=True
        )
        flag = jnp.sum(jnp.where(places == column, ocean, 0.0))
        values = jnp.where(lane_of == k, one, values)
        flags = jnp.where(iota((8, LANES), 1) == k, flag, flags)
        return values, flags

    values, flags = lax.fori_loop(
        0, here, gather, (jnp.zeros((members, LANES), F32), jnp.zeros((8, LANES), F32))
    )
    spare = jnp.zeros((LANES - members - 8, LANES), F32)
    rows = jnp.concatenate([values, flags, spare], axis=0).T
    width = members + 1
    lanes = iota((1, LANES), 1)
    pieces = [jnp.zeros((1, LANES), F32) for _ in range(packed.shape[1] // LANES)]
    for k in range(SLOTS):
        chunk, shift = divmod(k * width, LANES)
        row = rows[k : k + 1]
        row = jnp.where(lanes < width, row, 0.0)
        if shift:
            row = pltpu.roll(row, shift, 1)
        pieces[chunk] = pieces[chunk] + jnp.where(lanes >= shift, row, 0.0)
        if shift + width > LANES:
            pieces[chunk + 1] = pieces[chunk + 1] + jnp.where(lanes < shift, row, 0.0)
    packed[...] = jnp.concatenate(pieces, axis=1)


def index_kernel(
    columns, tile_s, tile_v, cells_v, start_v, span_v, index_v, reach_v, bounds_s, segments_s, rounds_s
):
    batches, obs = cells_v.shape
    devices = tile_s.shape[0]
    mine = tile_s[my_device()]

    cells = cells_v[...]
    tiles = (cells // columns).astype(F32)
    tile_columns = [as_column(tiles[b : b + 1]) for b in range(batches)]
    order = tile_v[...].astype(F32)
    order_columns = [as_column(order[h : h + 1]) for h in range(devices // LANES)]
    above = iota((obs, obs), 0) < iota((obs, obs), 1)
    ids = iota((obs, obs), 0).astype(F32)
    ranks = []
    for b in range(batches):
        same = [tile_columns[a] == tiles[b : b + 1] for a in range(b + 1)]
        same[b] = same[b] & above
        rank = sum(jnp.sum(jnp.where(s, 1.0, 0.0), axis=0, keepdims=True) for s in same)
        owner = sum(
            jnp.sum(
                jnp.where(order_columns[h] == tiles[b : b + 1], ids + float(h * LANES), 0.0),
                axis=0,
                keepdims=True,
            )
            for h in range(devices // LANES)
        )
        index_v[b : b + 1, :] = (rank * float(devices) + owner).astype(jnp.int32)
        ranks.append(rank)
    highest = jnp.max(jnp.concatenate(ranks, axis=0)).astype(jnp.int32)
    rounds_s[0] = highest // SLOTS + 1

    at = 0
    for b in range(batches - 1):
        begin = as_column(start_v[b : b + 1, :].astype(F32))
        end = begin + as_column(span_v[b : b + 1, :].astype(F32))
        for a in range(b + 1, batches):
            place = cells_v[a : a + 1, :].astype(F32)
            inside = (place >= begin) & (place < end)
            reach_v[:, at : at + obs] = jnp.where(inside, 1.0, 0.0)
            at += obs

    begin = start_v[...] - mine * columns
    edges = jnp.concatenate([begin, begin + span_v[...]], axis=0).astype(F32)
    edges = jnp.where(edges < float(columns), edges, BIG)
    bounds_s[0] = 0

    def next_edge(state):
        at, found = state
        later = jnp.min(jnp.where(edges > at.astype(F32), edges, BIG))
        at = jnp.minimum(later, float(columns)).astype(jnp.int32)
        bounds_s[found + 1] = at
        return at, found + 1

    _, found = lax.while_loop(lambda s: s[0] < columns, next_edge, (jnp.int32(0), jnp.int32(0)))
    segments_s[0] = found
    for k in range(GROUP):
        bounds_s[found + 1 + k] = columns


def split_kernel(prior, parts):
    stack, members, columns = prior.shape

    @pl.loop(0, stack)
    def _(v):
        block = prior[v]
        spread = block - jnp.sum(block, axis=0, keepdims=True) * (1.0 / members)
        high, low = two_parts(spread)
        parts[v, 0:members, :] = high
        parts[v, members : 2 * members, :] = low
        parts[v, 2 * members : 3 * members, :] = high
        parts[v, 3 * members :, :] = jnp.zeros((DEPTH - 3 * members, columns), BF16)


def place_kernel(members, turn_s, index_s, arrived, *refs):
    *before, out, rows, ordered = refs
    if before:
        ordered[...] = before[0][...].T
    devices = arrived.shape[0]
    width = members + 1
    lanes = iota((devices, LANES), 1)
    for k in range(SLOTS):
        chunk, shift = divmod(k * width, LANES)
        part = arrived[:, chunk * LANES : (chunk + 1) * LANES]
        if shift:
            part = pltpu.roll(part, LANES - shift, 1)
        if shift + width > LANES:
            after = arrived[:, (chunk + 1) * LANES : (chunk + 2) * LANES]
            after = pltpu.roll(after, LANES - shift, 1)
            part = jnp.where(lanes < LANES - shift, part, after)
        rows[k * devices : (k + 1) * devices, :] = jnp.where(lanes < width, part, 0.0)
    base = turn_s[0] * (SLOTS * devices)
    last = SLOTS * devices - 1

    @pl.loop(0, ordered.shape[0] // 16)
    def _(step):
        for inner in range(16):
            n = step * 16 + inner
            at = index_s[n] - base
            row = rows[pl.ds(jnp.clip(at, 0, last), 1), :]
            if before:
                row = jnp.where((at >= 0) & (at <= last), row, ordered[pl.ds(n, 1), :])
            ordered[pl.ds(n, 1), :] = row

    out[...] = ordered[...].T


def sweep_kernel(
    members,
    bounds_s,
    segments_s,
    tile_s,
    obs_v,
    start_v,
    span_v,
    gain_mean,
    gain_spread,
    ocean_v,
    reach,
    priors,
    split,
    prior,
    out,
    state,
    parts,
    values,
    weights_f,
    weights_p,
    anoms_p,
    maps_f,
    maps_p,
    sems,
):
    stack, _, columns = prior.shape
    batches, obs = obs_v.shape
    base = tile_s[my_device()] * columns
    chunks = columns // CHUNK

    def chunk(c):
        return pl.ds(pl.multiple_of(c * CHUNK, CHUNK), CHUNK)

    def loads(c):
        at = chunk(c)
        return (
            pltpu.make_async_copy(split.at[:, :, at], parts.at[:, :, at], sems.at[c]),
            pltpu.make_async_copy(prior.at[:, :, at], state.at[:, :, at], sems.at[chunks + c]),
        )

    for c in range(chunks):
        for load in loads(c):
            load.start()

    values[...] = priors[...]
    spare = jnp.zeros((LANES - members, obs), F32)
    reached = 0

    def mean_of(block):
        return jnp.sum(block, axis=0, keepdims=True) * (1.0 / members)

    for b in range(batches):
        mean = mean_of(values[0:members, b * obs : (b + 1) * obs])
        anomalies = values[0:members, b * obs : (b + 1) * obs] - mean
        innovation = jnp.broadcast_to(obs_v[b : b + 1, :] - mean, (members, obs))
        against = jnp.concatenate([innovation, anomalies], axis=1)
        gains = jnp.concatenate([gain_mean[b], -gain_spread[b]], axis=1)
        weights = exact_dot(against, gains, 1)
        scaled = jnp.concatenate([anomalies, spare], axis=0).T * (1.0 / (members - 1.0))
        if b + 1 < batches:
            later = values[0:members, (b + 1) * obs :]
            extent = later.shape[1]
            spread = later - mean_of(later)
            spread = jnp.concatenate(
                [spread, jnp.zeros((LANES - members, extent), F32)], axis=0
            )
            wet = values[members : members + 1, (b + 1) * obs :]
            gain = exact_dot(scaled, spread) * (reach[:, reached : reached + extent] * wet)
            values[0:members, (b + 1) * obs :] = later + exact_dot(weights, gain)
            reached += extent
        weights_f[b] = weights
        high, low = two_parts(weights)
        weights_p[b] = jnp.concatenate(
            [high, low, high, jnp.zeros((DEPTH - 3 * members, obs), BF16)], axis=0
        )
        wide = jnp.concatenate([-scaled, jnp.zeros_like(scaled)], axis=1)
        wide = wide + pltpu.roll(wide, members, 1) + pltpu.roll(wide, 2 * members, 1)
        high, low = two_parts(wide)
        anoms_p[b] = jnp.concatenate([high, high, low], axis=0)

    segments = segments_s[0]

    def store(c):
        at = chunk(c)
        return pltpu.make_async_copy(
            state.at[:, :, at], out.at[:, :, at], sems.at[2 * chunks + c]
        )

    wide_lane = iota((GROUP * members, DEPTH), 1)

    @pl.loop(0, pl.cdiv(segments, GROUP))
    def _(group):
        first = group * GROUP
        bounds = [bounds_s[first + k] for k in range(GROUP + 1)]
        for b in reversed(range(batches)):
            begin = start_v[b : b + 1, :]
            end = begin + span_v[b : b + 1, :]
            if b < batches - 1:
                grown = dot(maps_p[...], weights_p[b])
            pieces = []
            for k in range(GROUP):
                at = base + bounds[k]
                piece = weights_f[b]
                if b < batches - 1:
                    piece = piece + grown[k * members : (k + 1) * members]
                pieces.append(jnp.where((begin <= at) & (at < end), piece, 0.0))
            high, low = two_parts(jnp.concatenate(pieces, axis=0))
            maps = dot(jnp.concatenate([high, low, high], axis=1), anoms_p[b])
            maps = (maps_f[...] if b < batches - 1 else 0.0) - maps
            maps_f[...] = maps
            rest = maps - maps.astype(BF16).astype(F32)
            maps_p[...] = jnp.where(wide_lane < 2 * members, maps, rest).astype(BF16)

        @pl.loop(0, jnp.minimum(segments - first, GROUP))
        def _(k):
            low, high = bounds_s[first + k], bounds_s[first + k + 1]

            @pl.loop(low // CHUNK, pl.cdiv(high, CHUNK))
            def _(c):
                at = pl.multiple_of(c * CHUNK, CHUNK)
                place = at + iota((1, CHUNK), 1)
                inside = (place >= low) & (place < high)
                inside = inside & (ocean_v[0:1, pl.ds(at, CHUNK)] > 0)
                own_map = maps_p[pl.ds(pl.multiple_of(k * members, 16), members), :]

                @pl.when(low <= at)
                def _():
                    for load in loads(c):
                        load.wait()

                @pl.loop(0, stack, unroll=UNROLL)
                def _(v):
                    change = dot(own_map, parts[v, :, pl.ds(at, CHUNK)])
                    before = state[v, :, pl.ds(at, CHUNK)]
                    state[v, :, pl.ds(at, CHUNK)] = jnp.where(inside, before + change, before)

                @pl.when(high >= at + CHUNK)
                def _():
                    store(c).start()

    for c in range(columns // CHUNK):
        store(c).wait()


def per_device(
    prior,
    ocean_mask,
    tile_order,
    obs_cell,
    obs_stack,
    obs_values,
    window_start,
    window_span,
    gain_mean,
    gain_spread,
):
    members, stack, columns = prior.shape
    batches, obs = obs_cell.shape
    total = batches * obs
    devices = tile_order.shape[0]
    wide = -(-SLOTS * (members + 1) // LANES) * LANES
    smem = pl.BlockSpec(memory_space=pltpu.SMEM)
    vmem = pl.BlockSpec(memory_space=pltpu.VMEM)
    hbm = pl.BlockSpec(memory_space=pltpu.HBM)
    cells_flat = obs_cell.reshape(-1)
    stacks_flat = obs_stack.reshape(-1)
    tiles_2d = tile_order.reshape(-1, LANES)
    limit = 24 * 1024 * 1024

    params = pltpu.CompilerParams(vmem_limit_bytes=limit)
    by_stack = prior.transpose(1, 0, 2)

    def pick(turn):
        return pl.pallas_call(
            functools.partial(pick_kernel, columns),
            out_shape=jax.ShapeDtypeStruct((1, wide), F32),
            in_specs=[smem] * 4 + [vmem] * 2 + [hbm],
            out_specs=vmem,
            scratch_shapes=[
                pltpu.SMEM((SLOTS,), jnp.int32),
                pltpu.VMEM((SLOTS, members, LANES), F32),
                pltpu.SemaphoreType.DMA((SLOTS,)),
            ],
            compiler_params=params,
            name="pick",
        )(
            turn,
            tile_order,
            cells_flat,
            stacks_flat,
            obs_cell,
            ocean_mask.reshape(-1, LANES),
            by_stack,
        )

    def place(turn, index, packed, *before):
        sent = jnp.broadcast_to(packed[None], (devices, 1, wide))
        arrived = lax.all_to_all(sent, ROW_COL, 0, 0, tiled=True).reshape(devices, wide)
        return pl.pallas_call(
            functools.partial(place_kernel, members),
            out_shape=jax.ShapeDtypeStruct((LANES, total), F32),
            in_specs=[smem, smem, vmem] + [vmem] * len(before),
            out_specs=vmem,
            scratch_shapes=[
                pltpu.VMEM((SLOTS * devices, LANES), F32),
                pltpu.VMEM((total, LANES), F32),
            ],
            compiler_params=params,
            name="place",
        )(turn, index, arrived, *before)

    turn = jnp.zeros((1,), jnp.int32)
    packed = pick(turn)
    index, reach, bounds, segments, rounds = pl.pallas_call(
        functools.partial(index_kernel, columns),
        out_shape=(
            jax.ShapeDtypeStruct((batches, obs), jnp.int32),
            jax.ShapeDtypeStruct((obs, batches * (batches - 1) // 2 * obs), F32),
            jax.ShapeDtypeStruct((columns + 1 + GROUP,), jnp.int32),
            jax.ShapeDtypeStruct((1,), jnp.int32),
            jax.ShapeDtypeStruct((1,), jnp.int32),
        ),
        in_specs=[smem] + [vmem] * 4,
        out_specs=(vmem, vmem, smem, smem, smem),
        compiler_params=params,
        name="index",
    )(tile_order, tiles_2d, obs_cell, window_start, window_span)
    parts = pl.pallas_call(
        split_kernel,
        out_shape=jax.ShapeDtypeStruct((stack, DEPTH, columns), BF16),
        in_specs=[vmem],
        out_specs=vmem,
        compiler_params=params,
        name="split",
    )(by_stack)
    index = index.reshape(-1)
    values = place(turn, index, packed)

    def again(state):
        turn, before = state
        return turn + 1, place(turn, index, pick(turn), before)

    _, values = lax.while_loop(lambda s: (s[0] < rounds)[0], again, (turn + 1, values))

    posterior = pl.pallas_call(
        functools.partial(sweep_kernel, members),
        out_shape=jax.ShapeDtypeStruct((stack, members, columns), F32),
        in_specs=[smem] * 3 + [vmem] * 8 + [hbm] * 2,
        out_specs=hbm,
        scratch_shapes=[
            pltpu.VMEM((stack, members, columns), F32),
            pltpu.VMEM((stack, DEPTH, columns), BF16),
            pltpu.VMEM((LANES, total), F32),
            pltpu.VMEM((batches, members, obs), F32),
            pltpu.VMEM((batches, DEPTH, obs), BF16),
            pltpu.VMEM((batches, 3 * obs, DEPTH), BF16),
            pltpu.VMEM((GROUP * members, DEPTH), F32),
            pltpu.VMEM((GROUP * members, DEPTH), BF16),
            pltpu.SemaphoreType.DMA((3 * columns // CHUNK,)),
        ],
        compiler_params=pltpu.CompilerParams(vmem_limit_bytes=60 * 1024 * 1024),
        name="sweep",
    )(
        bounds,
        segments,
        tile_order,
        obs_values,
        window_start,
        window_span,
        gain_mean,
        gain_spread,
        ocean_mask.reshape(1, -1),
        reach,
        values,
        parts,
        by_stack,
    )
    return posterior.transpose(1, 0, 2)


def solution(mesh):
    in_specs = (P(None, None, ROW_COL), P(ROW_COL), P(), P(), P(), P(), P(), P(), P(), P())
    return jax.shard_map(
        per_device, mesh=mesh, in_specs=in_specs, out_specs=P(None, None, ROW_COL), check_vma=False
    )
```

```python
import functools

import jax
import jax.numpy as jnp
from jax import lax
from jax.experimental import pallas as pl
from jax.experimental.pallas import tpu as pltpu
from jax.sharding import Mesh
from jax.sharding import PartitionSpec as P

ROW_COL = ("row", "col_0", "col_1", "col_2")
FIRST = ("row", "col_2")
SECOND = ("col_0", "col_1")
HIGHEST = lax.Precision.HIGHEST
F32 = jnp.float32
BF16 = jnp.bfloat16

LANES = 128
SLOTS = 9
GROUP = 4
DEPTH = 256
CHUNK = 128
UNROLL = 30
BIG = 1e9


def iota(shape, dim):
    return lax.broadcasted_iota(jnp.int32, shape, dim)


def as_column(row):
    size = row.shape[-1]
    eye = iota((size, size), 0) == iota((size, size), 1)
    return jnp.sum(jnp.where(eye, row, 0.0), axis=1, keepdims=True)


def dot(a, b):
    return lax.dot_general(a, b, (((1,), (0,)), ((), ())), preferred_element_type=F32)


def exact_dot(a, b, contract=0):
    return lax.dot_general(
        a, b, (((1,), (contract,)), ((), ())), precision=HIGHEST, preferred_element_type=F32
    )


def two_parts(x):
    high = x.astype(BF16)
    return high, (x - high.astype(F32)).astype(BF16)


def my_device():
    device = 0
    for name in ROW_COL:
        device = device * lax.axis_size(name) + lax.axis_index(name)
    return device


def pick_kernel(
    columns, turn_s, tile_s, cells_s, stacks_s, cells_v, ocean_v, prior, packed, owned_s, held, sems
):
    batches, obs = cells_v.shape
    members = prior.shape[1]
    mine = tile_s[my_device()]
    first = turn_s[0] * SLOTS
    numbers = (iota((batches, obs), 0) * obs + iota((batches, obs), 1)).astype(F32)
    numbers = jnp.where(cells_v[...] // columns == mine, numbers, BIG)

    def fetch(k):
        n = owned_s[k]
        lane = pl.multiple_of(cells_s[n] % columns // LANES * LANES, LANES)
        return pltpu.make_async_copy(
            prior.at[stacks_s[n], :, pl.ds(lane, LANES)], held.at[k], sems.at[k]
        )

    def after(n):
        return jnp.min(jnp.where(numbers > n, numbers, BIG))

    def find(state):
        n, rank = state

        @pl.when(rank >= first)
        def _():
            owned_s[rank - first] = n.astype(jnp.int32)
            fetch(rank - first).start()

        return after(n), rank + 1

    _, found = lax.while_loop(
        lambda s: (s[0] < BIG) & (s[1] < first + SLOTS), find, (after(-1.0), jnp.int32(0))
    )
    here = jnp.maximum(found - first, 0)

    lane_of = iota((members, LANES), 1)
    places = iota((columns // LANES, LANES), 0) * LANES + iota((columns // LANES, LANES), 1)
    ocean = ocean_v[...].astype(F32)

    def gather(k, state):
        values, flags = state
        fetch(k).wait()
        column = cells_s[owned_s[k]] % columns
        one = jnp.sum(
            jnp.where(lane_of == column % LANES, held[k], 0.0), axis=1, keepdims=True
        )
        flag = jnp.sum(jnp.where(places == column, ocean, 0.0))
        values = jnp.where(lane_of == k, one, values)
        flags = jnp.where(iota((8, LANES), 1) == k, flag, flags)
        return values, flags

    values, flags = lax.fori_loop(
        0, here, gather, (jnp.zeros((members, LANES), F32), jnp.zeros((8, LANES), F32))
    )
    spare = jnp.zeros((LANES - members - 8, LANES), F32)
    rows = jnp.concatenate([values, flags, spare], axis=0).T
    width = members + 1
    lanes = iota((1, LANES), 1)
    pieces = [jnp.zeros((1, LANES), F32) for _ in range(packed.shape[1] // LANES)]
    for k in range(SLOTS):
        chunk, shift = divmod(k * width, LANES)
        row = rows[k : k + 1]
        row = jnp.where(lanes < width, row, 0.0)
        if shift:
            row = pltpu.roll(row, shift, 1)
        pieces[chunk] = pieces[chunk] + jnp.where(lanes >= shift, row, 0.0)
        if shift + width > LANES:
            pieces[chunk + 1] = pieces[chunk + 1] + jnp.where(lanes < shift, row, 0.0)
    packed[...] = jnp.concatenate(pieces, axis=1)


def index_kernel(
    columns, tile_s, tile_v, cells_v, start_v, span_v, index_v, reach_v, bounds_s, segments_s, rounds_s
):
    batches, obs = cells_v.shape
    devices = tile_s.shape[0]
    mine = tile_s[my_device()]

    cells = cells_v[...]
    tiles = (cells // columns).astype(F32)
    tile_columns = [as_column(tiles[b : b + 1]) for b in range(batches)]
    order = tile_v[...].astype(F32)
    order_columns = [as_column(order[h : h + 1]) for h in range(devices // LANES)]
    above = iota((obs, obs), 0) < iota((obs, obs), 1)
    cores = lax.axis_size("col_2")
    per_row = devices // lax.axis_size("row")
    per_first = cores * lax.axis_size("row")

    def arrival(device):
        row, rest = device // per_row, device % per_row
        return (rest // cores) * per_first + row * cores + rest % cores

    arrivals = [
        arrival(iota((obs, obs), 0) + h * LANES).astype(F32) for h in range(devices // LANES)
    ]
    ranks = []
    for b in range(batches):
        same = [tile_columns[a] == tiles[b : b + 1] for a in range(b + 1)]
        same[b] = same[b] & above
        rank = sum(jnp.sum(jnp.where(s, 1.0, 0.0), axis=0, keepdims=True) for s in same)
        owner = sum(
            jnp.sum(
                jnp.where(order_columns[h] == tiles[b : b + 1], arrivals[h], 0.0),
                axis=0,
                keepdims=True,
            )
            for h in range(devices // LANES)
        )
        index_v[b : b + 1, :] = (rank * float(devices) + owner).astype(jnp.int32)
        ranks.append(rank)
    highest = jnp.max(jnp.concatenate(ranks, axis=0)).astype(jnp.int32)
    rounds_s[0] = highest // SLOTS + 1

    at = 0
    for b in range(batches - 1):
        begin = as_column(start_v[b : b + 1, :].astype(F32))
        end = begin + as_column(span_v[b : b + 1, :].astype(F32))
        for a in range(b + 1, batches):
            place = cells_v[a : a + 1, :].astype(F32)
            inside = (place >= begin) & (place < end)
            reach_v[:, at : at + obs] = jnp.where(inside, 1.0, 0.0)
            at += obs

    begin = start_v[...] - mine * columns
    edges = jnp.concatenate([begin, begin + span_v[...]], axis=0).astype(F32)
    edges = jnp.where(edges < float(columns), edges, BIG)
    bounds_s[0] = 0

    def next_edge(state):
        at, found = state
        later = jnp.min(jnp.where(edges > at.astype(F32), edges, BIG))
        at = jnp.minimum(later, float(columns)).astype(jnp.int32)
        bounds_s[found + 1] = at
        return at, found + 1

    _, found = lax.while_loop(lambda s: s[0] < columns, next_edge, (jnp.int32(0), jnp.int32(0)))
    segments_s[0] = found
    for k in range(GROUP):
        bounds_s[found + 1 + k] = columns


def split_kernel(prior, parts):
    stack, members, columns = prior.shape

    @pl.loop(0, stack)
    def _(v):
        block = prior[v]
        spread = block - jnp.sum(block, axis=0, keepdims=True) * (1.0 / members)
        high, low = two_parts(spread)
        parts[v, 0:members, :] = high
        parts[v, members : 2 * members, :] = low
        parts[v, 2 * members : 3 * members, :] = high
        parts[v, 3 * members :, :] = jnp.zeros((DEPTH - 3 * members, columns), BF16)


def place_kernel(members, turn_s, index_s, arrived, *refs):
    *before, out, rows, ordered = refs
    if before:
        ordered[...] = before[0][...].T
    devices = arrived.shape[0]
    width = members + 1
    lanes = iota((devices, LANES), 1)
    for k in range(SLOTS):
        chunk, shift = divmod(k * width, LANES)
        part = arrived[:, chunk * LANES : (chunk + 1) * LANES]
        if shift:
            part = pltpu.roll(part, LANES - shift, 1)
        if shift + width > LANES:
            after = arrived[:, (chunk + 1) * LANES : (chunk + 2) * LANES]
            after = pltpu.roll(after, LANES - shift, 1)
            part = jnp.where(lanes < LANES - shift, part, after)
        rows[k * devices : (k + 1) * devices, :] = jnp.where(lanes < width, part, 0.0)
    base = turn_s[0] * (SLOTS * devices)
    last = SLOTS * devices - 1

    @pl.loop(0, ordered.shape[0] // 16)
    def _(step):
        for inner in range(16):
            n = step * 16 + inner
            at = index_s[n] - base
            row = rows[pl.ds(jnp.clip(at, 0, last), 1), :]
            if before:
                row = jnp.where((at >= 0) & (at <= last), row, ordered[pl.ds(n, 1), :])
            ordered[pl.ds(n, 1), :] = row

    out[...] = ordered[...].T


def sweep_kernel(
    members,
    bounds_s,
    segments_s,
    tile_s,
    obs_v,
    start_v,
    span_v,
    gain_mean,
    gain_spread,
    ocean_v,
    reach,
    priors,
    split,
    prior,
    out,
    state,
    parts,
    values,
    weights_f,
    weights_p,
    anoms_p,
    maps_f,
    maps_p,
    sems,
):
    stack, _, columns = prior.shape
    batches, obs = obs_v.shape
    base = tile_s[my_device()] * columns
    chunks = columns // CHUNK

    def chunk(c):
        return pl.ds(pl.multiple_of(c * CHUNK, CHUNK), CHUNK)

    def loads(c):
        at = chunk(c)
        return (
            pltpu.make_async_copy(split.at[:, :, at], parts.at[:, :, at], sems.at[c]),
            pltpu.make_async_copy(prior.at[:, :, at], state.at[:, :, at], sems.at[chunks + c]),
        )

    for c in range(chunks):
        for load in loads(c):
            load.start()

    values[...] = priors[...]
    spare = jnp.zeros((LANES - members, obs), F32)
    reached = 0

    def mean_of(block):
        return jnp.sum(block, axis=0, keepdims=True) * (1.0 / members)

    for b in range(batches):
        mean = mean_of(values[0:members, b * obs : (b + 1) * obs])
        anomalies = values[0:members, b * obs : (b + 1) * obs] - mean
        innovation = jnp.broadcast_to(obs_v[b : b + 1, :] - mean, (members, obs))
        against = jnp.concatenate([innovation, anomalies], axis=1)
        gains = jnp.concatenate([gain_mean[b], -gain_spread[b]], axis=1)
        weights = exact_dot(against, gains, 1)
        scaled = jnp.concatenate([anomalies, spare], axis=0).T * (1.0 / (members - 1.0))
        if b + 1 < batches:
            later = values[0:members, (b + 1) * obs :]
            extent = later.shape[1]
            spread = later - mean_of(later)
            spread = jnp.concatenate(
                [spread, jnp.zeros((LANES - members, extent), F32)], axis=0
            )
            wet = values[members : members + 1, (b + 1) * obs :]
            gain = exact_dot(scaled, spread) * (reach[:, reached : reached + extent] * wet)
            values[0:members, (b + 1) * obs :] = later + exact_dot(weights, gain)
            reached += extent
        weights_f[b] = weights
        high, low = two_parts(weights)
        weights_p[b] = jnp.concatenate(
            [high, low, high, jnp.zeros((DEPTH - 3 * members, obs), BF16)], axis=0
        )
        wide = jnp.concatenate([-scaled, jnp.zeros_like(scaled)], axis=1)
        wide = wide + pltpu.roll(wide, members, 1) + pltpu.roll(wide, 2 * members, 1)
        high, low = two_parts(wide)
        anoms_p[b] = jnp.concatenate([high, high, low], axis=0)

    segments = segments_s[0]

    def store(c):
        at = chunk(c)
        return pltpu.make_async_copy(
            state.at[:, :, at], out.at[:, :, at], sems.at[2 * chunks + c]
        )

    wide_lane = iota((GROUP * members, DEPTH), 1)

    @pl.loop(0, pl.cdiv(segments, GROUP))
    def _(group):
        first = group * GROUP
        bounds = [bounds_s[first + k] for k in range(GROUP + 1)]
        for b in reversed(range(batches)):
            begin = start_v[b : b + 1, :]
            end = begin + span_v[b : b + 1, :]
            if b < batches - 1:
                grown = dot(maps_p[...], weights_p[b])
            pieces = []
            for k in range(GROUP):
                at = base + bounds[k]
                piece = weights_f[b]
                if b < batches - 1:
                    piece = piece + grown[k * members : (k + 1) * members]
                pieces.append(jnp.where((begin <= at) & (at < end), piece, 0.0))
            high, low = two_parts(jnp.concatenate(pieces, axis=0))
            maps = dot(jnp.concatenate([high, low, high], axis=1), anoms_p[b])
            maps = (maps_f[...] if b < batches - 1 else 0.0) - maps
            maps_f[...] = maps
            rest = maps - maps.astype(BF16).astype(F32)
            maps_p[...] = jnp.where(wide_lane < 2 * members, maps, rest).astype(BF16)

        @pl.loop(0, jnp.minimum(segments - first, GROUP))
        def _(k):
            low, high = bounds_s[first + k], bounds_s[first + k + 1]

            @pl.loop(low // CHUNK, pl.cdiv(high, CHUNK))
            def _(c):
                at = pl.multiple_of(c * CHUNK, CHUNK)
                place = at + iota((1, CHUNK), 1)
                inside = (place >= low) & (place < high)
                inside = inside & (ocean_v[0:1, pl.ds(at, CHUNK)] > 0)
                own_map = maps_p[pl.ds(pl.multiple_of(k * members, 16), members), :]

                @pl.when(low <= at)
                def _():
                    for load in loads(c):
                        load.wait()

                @pl.loop(0, stack, unroll=UNROLL)
                def _(v):
                    change = dot(own_map, parts[v, :, pl.ds(at, CHUNK)])
                    before = state[v, :, pl.ds(at, CHUNK)]
                    state[v, :, pl.ds(at, CHUNK)] = jnp.where(inside, before + change, before)

                @pl.when(high >= at + CHUNK)
                def _():
                    store(c).start()

    for c in range(columns // CHUNK):
        store(c).wait()


def per_device(
    prior,
    ocean_mask,
    tile_order,
    obs_cell,
    obs_stack,
    obs_values,
    window_start,
    window_span,
    gain_mean,
    gain_spread,
):
    members, stack, columns = prior.shape
    batches, obs = obs_cell.shape
    total = batches * obs
    devices = tile_order.shape[0]
    wide = -(-SLOTS * (members + 1) // LANES) * LANES
    smem = pl.BlockSpec(memory_space=pltpu.SMEM)
    vmem = pl.BlockSpec(memory_space=pltpu.VMEM)
    hbm = pl.BlockSpec(memory_space=pltpu.HBM)
    cells_flat = obs_cell.reshape(-1)
    stacks_flat = obs_stack.reshape(-1)
    tiles_2d = tile_order.reshape(-1, LANES)
    limit = 24 * 1024 * 1024

    params = pltpu.CompilerParams(vmem_limit_bytes=limit)
    by_stack = prior.transpose(1, 0, 2)

    def pick(turn):
        return pl.pallas_call(
            functools.partial(pick_kernel, columns),
            out_shape=jax.ShapeDtypeStruct((1, wide), F32),
            in_specs=[smem] * 4 + [vmem] * 2 + [hbm],
            out_specs=vmem,
            scratch_shapes=[
                pltpu.SMEM((SLOTS,), jnp.int32),
                pltpu.VMEM((SLOTS, members, LANES), F32),
                pltpu.SemaphoreType.DMA((SLOTS,)),
            ],
            compiler_params=params,
            name="pick",
        )(
            turn,
            tile_order,
            cells_flat,
            stacks_flat,
            obs_cell,
            ocean_mask.reshape(-1, LANES),
            by_stack,
        )

    def place(turn, index, packed, *before):
        near = lax.axis_size(FIRST)
        sent = jnp.broadcast_to(packed[None], (near, 1, wide))
        group = lax.all_to_all(sent, FIRST, 0, 0, tiled=True).reshape(near, wide)
        sent = jnp.broadcast_to(group[None], (devices // near, near, wide))
        arrived = lax.all_to_all(sent, SECOND, 0, 0, tiled=True).reshape(devices, wide)
        return pl.pallas_call(
            functools.partial(place_kernel, members),
            out_shape=jax.ShapeDtypeStruct((LANES, total), F32),
            in_specs=[smem, smem, vmem] + [vmem] * len(before),
            out_specs=vmem,
            scratch_shapes=[
                pltpu.VMEM((SLOTS * devices, LANES), F32),
                pltpu.VMEM((total, LANES), F32),
            ],
            compiler_params=params,
            name="place",
        )(turn, index, arrived, *before)

    turn = jnp.zeros((1,), jnp.int32)
    packed = pick(turn)
    index, reach, bounds, segments, rounds = pl.pallas_call(
        functools.partial(index_kernel, columns),
        out_shape=(
            jax.ShapeDtypeStruct((batches, obs), jnp.int32),
            jax.ShapeDtypeStruct((obs, batches * (batches - 1) // 2 * obs), F32),
            jax.ShapeDtypeStruct((columns + 1 + GROUP,), jnp.int32),
            jax.ShapeDtypeStruct((1,), jnp.int32),
            jax.ShapeDtypeStruct((1,), jnp.int32),
        ),
        in_specs=[smem] + [vmem] * 4,
        out_specs=(vmem, vmem, smem, smem, smem),
        compiler_params=params,
        name="index",
    )(tile_order, tiles_2d, obs_cell, window_start, window_span)
    parts = pl.pallas_call(
        split_kernel,
        out_shape=jax.ShapeDtypeStruct((stack, DEPTH, columns), BF16),
        in_specs=[vmem],
        out_specs=vmem,
        compiler_params=params,
        name="split",
    )(by_stack)
    index = index.reshape(-1)
    values = place(turn, index, packed)

    def again(state):
        turn, before = state
        return turn + 1, place(turn, index, pick(turn), before)

    _, values = lax.while_loop(lambda s: (s[0] < rounds)[0], again, (turn + 1, values))

    posterior = pl.pallas_call(
        functools.partial(sweep_kernel, members),
        out_shape=jax.ShapeDtypeStruct((stack, members, columns), F32),
        in_specs=[smem] * 3 + [vmem] * 8 + [hbm] * 2,
        out_specs=hbm,
        scratch_shapes=[
            pltpu.VMEM((stack, members, columns), F32),
            pltpu.VMEM((stack, DEPTH, columns), BF16),
            pltpu.VMEM((LANES, total), F32),
            pltpu.VMEM((batches, members, obs), F32),
            pltpu.VMEM((batches, DEPTH, obs), BF16),
            pltpu.VMEM((batches, 3 * obs, DEPTH), BF16),
            pltpu.VMEM((GROUP * members, DEPTH), F32),
            pltpu.VMEM((GROUP * members, DEPTH), BF16),
            pltpu.SemaphoreType.DMA((3 * columns // CHUNK,)),
        ],
        compiler_params=pltpu.CompilerParams(vmem_limit_bytes=60 * 1024 * 1024),
        name="sweep",
    )(
        bounds,
        segments,
        tile_order,
        obs_values,
        window_start,
        window_span,
        gain_mean,
        gain_spread,
        ocean_mask.reshape(1, -1),
        reach,
        values,
        parts,
        by_stack,
    )
    return posterior.transpose(1, 0, 2)


def solution(mesh):
    split = Mesh(mesh.devices.reshape(mesh.shape["row"], 4, 4, 2), ROW_COL)
    in_specs = (P(None, None, ROW_COL), P(ROW_COL), P(), P(), P(), P(), P(), P(), P(), P())
    return jax.shard_map(
        per_device, mesh=split, in_specs=in_specs, out_specs=P(None, None, ROW_COL), check_vma=False
    )
```

```python
import functools

import jax
import jax.numpy as jnp
from jax import lax
from jax.experimental import pallas as pl
from jax.experimental.pallas import tpu as pltpu
from jax.sharding import Mesh
from jax.sharding import PartitionSpec as P

ROW_COL = ("row", "col_0", "col_1", "col_2")
FIRST = ("row", "col_2")
SECOND = ("col_0", "col_1")
HIGHEST = lax.Precision.HIGHEST
F32 = jnp.float32
BF16 = jnp.bfloat16

LANES = 128
SLOTS = 9
GROUP = 4
DEPTH = 256
CHUNK = 128
UNROLL = 30
BIG = 1e9


def iota(shape, dim):
    return lax.broadcasted_iota(jnp.int32, shape, dim)


def as_column(row):
    size = row.shape[-1]
    eye = iota((size, size), 0) == iota((size, size), 1)
    return jnp.sum(jnp.where(eye, row, 0.0), axis=1, keepdims=True)


def dot(a, b):
    return lax.dot_general(a, b, (((1,), (0,)), ((), ())), preferred_element_type=F32)


def exact_dot(a, b, contract=0):
    return lax.dot_general(
        a, b, (((1,), (contract,)), ((), ())), precision=HIGHEST, preferred_element_type=F32
    )


def two_parts(x):
    high = x.astype(BF16)
    return high, (x - high.astype(F32)).astype(BF16)


def my_device():
    device = 0
    for name in ROW_COL:
        device = device * lax.axis_size(name) + lax.axis_index(name)
    return device


def pick_kernel(
    columns, turn_s, tile_s, cells_s, stacks_s, cells_v, ocean_v, prior, packed, owned_s, held, sems
):
    batches, obs = cells_v.shape
    members = prior.shape[1]
    mine = tile_s[my_device()]
    first = turn_s[0] * SLOTS
    numbers = (iota((batches, obs), 0) * obs + iota((batches, obs), 1)).astype(F32)
    numbers = jnp.where(cells_v[...] // columns == mine, numbers, BIG)

    def fetch(k):
        n = owned_s[k]
        lane = pl.multiple_of(cells_s[n] % columns // LANES * LANES, LANES)
        return pltpu.make_async_copy(
            prior.at[stacks_s[n], :, pl.ds(lane, LANES)], held.at[k], sems.at[k]
        )

    def after(n):
        return jnp.min(jnp.where(numbers > n, numbers, BIG))

    def find(state):
        n, rank = state

        @pl.when(rank >= first)
        def _():
            owned_s[rank - first] = n.astype(jnp.int32)
            fetch(rank - first).start()

        return after(n), rank + 1

    _, found = lax.while_loop(
        lambda s: (s[0] < BIG) & (s[1] < first + SLOTS), find, (after(-1.0), jnp.int32(0))
    )
    here = jnp.maximum(found - first, 0)

    lane_of = iota((members, LANES), 1)
    places = iota((columns // LANES, LANES), 0) * LANES + iota((columns // LANES, LANES), 1)
    ocean = ocean_v[...].astype(F32)

    def gather(k, state):
        values, flags = state
        fetch(k).wait()
        column = cells_s[owned_s[k]] % columns
        one = jnp.sum(
            jnp.where(lane_of == column % LANES, held[k], 0.0), axis=1, keepdims=True
        )
        flag = jnp.sum(jnp.where(places == column, ocean, 0.0))
        values = jnp.where(lane_of == k, one, values)
        flags = jnp.where(iota((8, LANES), 1) == k, flag, flags)
        return values, flags

    values, flags = lax.fori_loop(
        0, here, gather, (jnp.zeros((members, LANES), F32), jnp.zeros((8, LANES), F32))
    )
    spare = jnp.zeros((LANES - members - 8, LANES), F32)
    rows = jnp.concatenate([values, flags, spare], axis=0).T
    width = members + 1
    lanes = iota((1, LANES), 1)
    pieces = [jnp.zeros((1, LANES), F32) for _ in range(packed.shape[1] // LANES)]
    for k in range(SLOTS):
        chunk, shift = divmod(k * width, LANES)
        row = rows[k : k + 1]
        row = jnp.where(lanes < width, row, 0.0)
        if shift:
            row = pltpu.roll(row, shift, 1)
        pieces[chunk] = pieces[chunk] + jnp.where(lanes >= shift, row, 0.0)
        if shift + width > LANES:
            pieces[chunk + 1] = pieces[chunk + 1] + jnp.where(lanes < shift, row, 0.0)
    packed[...] = jnp.concatenate(pieces, axis=1)


def index_kernel(
    columns, tile_s, tile_v, cells_v, start_v, span_v, index_v, reach_v, bounds_s, segments_s, rounds_s
):
    batches, obs = cells_v.shape
    devices = tile_s.shape[0]
    mine = tile_s[my_device()]

    cells = cells_v[...]
    tiles = (cells // columns).astype(F32)
    tile_columns = [as_column(tiles[b : b + 1]) for b in range(batches)]
    order = tile_v[...].astype(F32)
    order_columns = [as_column(order[h : h + 1]) for h in range(devices // LANES)]
    above = iota((obs, obs), 0) < iota((obs, obs), 1)
    cores = lax.axis_size("col_2")
    per_row = devices // lax.axis_size("row")
    per_first = cores * lax.axis_size("row")

    def arrival(device):
        row, rest = device // per_row, device % per_row
        return (rest // cores) * per_first + row * cores + rest % cores

    arrivals = [
        arrival(iota((obs, obs), 0) + h * LANES).astype(F32) for h in range(devices // LANES)
    ]
    ranks = []
    for b in range(batches):
        same = [tile_columns[a] == tiles[b : b + 1] for a in range(b + 1)]
        same[b] = same[b] & above
        rank = sum(jnp.sum(jnp.where(s, 1.0, 0.0), axis=0, keepdims=True) for s in same)
        owner = sum(
            jnp.sum(
                jnp.where(order_columns[h] == tiles[b : b + 1], arrivals[h], 0.0),
                axis=0,
                keepdims=True,
            )
            for h in range(devices // LANES)
        )
        index_v[b : b + 1, :] = (rank * float(devices) + owner).astype(jnp.int32)
        ranks.append(rank)
    highest = jnp.max(jnp.concatenate(ranks, axis=0)).astype(jnp.int32)
    rounds_s[0] = highest // SLOTS + 1

    at = 0
    for b in range(batches - 1):
        begin = as_column(start_v[b : b + 1, :].astype(F32))
        end = begin + as_column(span_v[b : b + 1, :].astype(F32))
        for a in range(b + 1, batches):
            place = cells_v[a : a + 1, :].astype(F32)
            inside = (place >= begin) & (place < end)
            reach_v[:, at : at + obs] = jnp.where(inside, 1.0, 0.0)
            at += obs

    begin = start_v[...] - mine * columns
    edges = jnp.concatenate([begin, begin + span_v[...]], axis=0).astype(F32)
    edges = jnp.where(edges < float(columns), edges, BIG)
    bounds_s[0] = 0

    def next_edge(state):
        at, found = state
        later = jnp.min(jnp.where(edges > at.astype(F32), edges, BIG))
        at = jnp.minimum(later, float(columns)).astype(jnp.int32)
        bounds_s[found + 1] = at
        return at, found + 1

    _, found = lax.while_loop(lambda s: s[0] < columns, next_edge, (jnp.int32(0), jnp.int32(0)))
    segments_s[0] = found
    for k in range(GROUP):
        bounds_s[found + 1 + k] = columns


def split_kernel(prior, parts):
    stack, members, columns = prior.shape

    @pl.loop(0, stack)
    def _(v):
        block = prior[v]
        spread = block - jnp.sum(block, axis=0, keepdims=True) * (1.0 / members)
        high, low = two_parts(spread)
        parts[v, 0:members, :] = high
        parts[v, members : 2 * members, :] = low
        parts[v, 2 * members : 3 * members, :] = high
        parts[v, 3 * members :, :] = jnp.zeros((DEPTH - 3 * members, columns), BF16)


def place_kernel(members, turn_s, index_s, arrived, *refs):
    *before, out, rows, ordered = refs
    if before:
        ordered[...] = before[0][...].T
    devices = arrived.shape[0]
    width = members + 1
    lanes = iota((devices, LANES), 1)
    for k in range(SLOTS):
        chunk, shift = divmod(k * width, LANES)
        part = arrived[:, chunk * LANES : (chunk + 1) * LANES]
        if shift:
            part = pltpu.roll(part, LANES - shift, 1)
        if shift + width > LANES:
            after = arrived[:, (chunk + 1) * LANES : (chunk + 2) * LANES]
            after = pltpu.roll(after, LANES - shift, 1)
            part = jnp.where(lanes < LANES - shift, part, after)
        rows[k * devices : (k + 1) * devices, :] = jnp.where(lanes < width, part, 0.0)
    base = turn_s[0] * (SLOTS * devices)
    last = SLOTS * devices - 1

    @pl.loop(0, ordered.shape[0] // 64)
    def _(step):
        for inner in range(64):
            n = step * 64 + inner
            at = index_s[n] - base
            row = rows[pl.ds(jnp.clip(at, 0, last), 1), :]
            if before:
                row = jnp.where((at >= 0) & (at <= last), row, ordered[pl.ds(n, 1), :])
            ordered[pl.ds(n, 1), :] = row

    out[...] = ordered[...].T


def sweep_kernel(
    members,
    bounds_s,
    segments_s,
    tile_s,
    obs_v,
    start_v,
    span_v,
    gain_mean,
    gain_spread,
    ocean_v,
    reach,
    priors,
    split,
    prior,
    out,
    state,
    parts,
    values,
    weights_f,
    weights_p,
    anoms_p,
    maps_f,
    maps_p,
    sems,
):
    stack, _, columns = prior.shape
    batches, obs = obs_v.shape
    base = tile_s[my_device()] * columns
    chunks = columns // CHUNK

    def chunk(c):
        return pl.ds(pl.multiple_of(c * CHUNK, CHUNK), CHUNK)

    def loads(c):
        at = chunk(c)
        return (
            pltpu.make_async_copy(split.at[:, :, at], parts.at[:, :, at], sems.at[c]),
            pltpu.make_async_copy(prior.at[:, :, at], state.at[:, :, at], sems.at[chunks + c]),
        )

    for c in range(chunks):
        for load in loads(c):
            load.start()

    values[...] = priors[...]
    spare = jnp.zeros((LANES - members, obs), F32)
    reached = 0

    def mean_of(block):
        return jnp.sum(block, axis=0, keepdims=True) * (1.0 / members)

    for b in range(batches):
        mean = mean_of(values[0:members, b * obs : (b + 1) * obs])
        anomalies = values[0:members, b * obs : (b + 1) * obs] - mean
        innovation = jnp.broadcast_to(obs_v[b : b + 1, :] - mean, (members, obs))
        against = jnp.concatenate([innovation, anomalies], axis=1)
        gains = jnp.concatenate([gain_mean[b], -gain_spread[b]], axis=1)
        weights = exact_dot(against, gains, 1)
        scaled = jnp.concatenate([anomalies, spare], axis=0).T * (1.0 / (members - 1.0))
        if b + 1 < batches:
            later = values[0:members, (b + 1) * obs :]
            extent = later.shape[1]
            spread = later - mean_of(later)
            spread = jnp.concatenate(
                [spread, jnp.zeros((LANES - members, extent), F32)], axis=0
            )
            wet = values[members : members + 1, (b + 1) * obs :]
            gain = exact_dot(scaled, spread) * (reach[:, reached : reached + extent] * wet)
            values[0:members, (b + 1) * obs :] = later + exact_dot(weights, gain)
            reached += extent
        weights_f[b] = weights
        high, low = two_parts(weights)
        weights_p[b] = jnp.concatenate(
            [high, low, high, jnp.zeros((DEPTH - 3 * members, obs), BF16)], axis=0
        )
        wide = jnp.concatenate([-scaled, jnp.zeros_like(scaled)], axis=1)
        wide = wide + pltpu.roll(wide, members, 1) + pltpu.roll(wide, 2 * members, 1)
        high, low = two_parts(wide)
        anoms_p[b] = jnp.concatenate([high, high, low], axis=0)

    segments = segments_s[0]

    def store(c):
        at = chunk(c)
        return pltpu.make_async_copy(
            state.at[:, :, at], out.at[:, :, at], sems.at[2 * chunks + c]
        )

    wide_lane = iota((GROUP * members, DEPTH), 1)

    @pl.loop(0, pl.cdiv(segments, GROUP))
    def _(group):
        first = group * GROUP
        bounds = [bounds_s[first + k] for k in range(GROUP + 1)]
        for b in reversed(range(batches)):
            begin = start_v[b : b + 1, :]
            end = begin + span_v[b : b + 1, :]
            if b < batches - 1:
                grown = dot(maps_p[...], weights_p[b])
            pieces = []
            for k in range(GROUP):
                at = base + bounds[k]
                piece = weights_f[b]
                if b < batches - 1:
                    piece = piece + grown[k * members : (k + 1) * members]
                pieces.append(jnp.where((begin <= at) & (at < end), piece, 0.0))
            high, low = two_parts(jnp.concatenate(pieces, axis=0))
            maps = dot(jnp.concatenate([high, low, high], axis=1), anoms_p[b])
            maps = (maps_f[...] if b < batches - 1 else 0.0) - maps
            maps_f[...] = maps
            rest = maps - maps.astype(BF16).astype(F32)
            maps_p[...] = jnp.where(wide_lane < 2 * members, maps, rest).astype(BF16)

        @pl.loop(0, jnp.minimum(segments - first, GROUP))
        def _(k):
            low, high = bounds_s[first + k], bounds_s[first + k + 1]

            @pl.loop(low // CHUNK, pl.cdiv(high, CHUNK))
            def _(c):
                at = pl.multiple_of(c * CHUNK, CHUNK)
                place = at + iota((1, CHUNK), 1)
                inside = (place >= low) & (place < high)
                inside = inside & (ocean_v[0:1, pl.ds(at, CHUNK)] > 0)
                own_map = maps_p[pl.ds(pl.multiple_of(k * members, 16), members), :]

                @pl.when(low <= at)
                def _():
                    for load in loads(c):
                        load.wait()

                @pl.loop(0, stack, unroll=UNROLL)
                def _(v):
                    change = dot(own_map, parts[v, :, pl.ds(at, CHUNK)])
                    before = state[v, :, pl.ds(at, CHUNK)]
                    state[v, :, pl.ds(at, CHUNK)] = jnp.where(inside, before + change, before)

                @pl.when(high >= at + CHUNK)
                def _():
                    store(c).start()

    for c in range(columns // CHUNK):
        store(c).wait()


def per_device(
    prior,
    ocean_mask,
    tile_order,
    obs_cell,
    obs_stack,
    obs_values,
    window_start,
    window_span,
    gain_mean,
    gain_spread,
):
    members, stack, columns = prior.shape
    batches, obs = obs_cell.shape
    total = batches * obs
    devices = tile_order.shape[0]
    wide = -(-SLOTS * (members + 1) // LANES) * LANES
    smem = pl.BlockSpec(memory_space=pltpu.SMEM)
    vmem = pl.BlockSpec(memory_space=pltpu.VMEM)
    hbm = pl.BlockSpec(memory_space=pltpu.HBM)
    cells_flat = obs_cell.reshape(-1)
    stacks_flat = obs_stack.reshape(-1)
    tiles_2d = tile_order.reshape(-1, LANES)
    limit = 24 * 1024 * 1024

    params = pltpu.CompilerParams(vmem_limit_bytes=limit)
    by_stack = prior.transpose(1, 0, 2)

    def pick(turn):
        return pl.pallas_call(
            functools.partial(pick_kernel, columns),
            out_shape=jax.ShapeDtypeStruct((1, wide), F32),
            in_specs=[smem] * 4 + [vmem] * 2 + [hbm],
            out_specs=vmem,
            scratch_shapes=[
                pltpu.SMEM((SLOTS,), jnp.int32),
                pltpu.VMEM((SLOTS, members, LANES), F32),
                pltpu.SemaphoreType.DMA((SLOTS,)),
            ],
            compiler_params=params,
            name="pick",
        )(
            turn,
            tile_order,
            cells_flat,
            stacks_flat,
            obs_cell,
            ocean_mask.reshape(-1, LANES),
            by_stack,
        )

    def place(turn, index, packed, *before):
        near = lax.axis_size(FIRST)
        sent = jnp.broadcast_to(packed[None], (near, 1, wide))
        group = lax.all_to_all(sent, FIRST, 0, 0, tiled=True).reshape(near, wide)
        sent = jnp.broadcast_to(group[None], (devices // near, near, wide))
        arrived = lax.all_to_all(sent, SECOND, 0, 0, tiled=True).reshape(devices, wide)
        return pl.pallas_call(
            functools.partial(place_kernel, members),
            out_shape=jax.ShapeDtypeStruct((LANES, total), F32),
            in_specs=[smem, smem, vmem] + [vmem] * len(before),
            out_specs=vmem,
            scratch_shapes=[
                pltpu.VMEM((SLOTS * devices, LANES), F32),
                pltpu.VMEM((total, LANES), F32),
            ],
            compiler_params=params,
            name="place",
        )(turn, index, arrived, *before)

    turn = jnp.zeros((1,), jnp.int32)
    packed = pick(turn)
    index, reach, bounds, segments, rounds = pl.pallas_call(
        functools.partial(index_kernel, columns),
        out_shape=(
            jax.ShapeDtypeStruct((batches, obs), jnp.int32),
            jax.ShapeDtypeStruct((obs, batches * (batches - 1) // 2 * obs), F32),
            jax.ShapeDtypeStruct((columns + 1 + GROUP,), jnp.int32),
            jax.ShapeDtypeStruct((1,), jnp.int32),
            jax.ShapeDtypeStruct((1,), jnp.int32),
        ),
        in_specs=[smem] + [vmem] * 4,
        out_specs=(vmem, vmem, smem, smem, smem),
        compiler_params=params,
        name="index",
    )(tile_order, tiles_2d, obs_cell, window_start, window_span)
    parts = pl.pallas_call(
        split_kernel,
        out_shape=jax.ShapeDtypeStruct((stack, DEPTH, columns), BF16),
        in_specs=[vmem],
        out_specs=vmem,
        compiler_params=params,
        name="split",
    )(by_stack)
    index = index.reshape(-1)
    values = place(turn, index, packed)

    def again(state):
        turn, before = state
        return turn + 1, place(turn, index, pick(turn), before)

    _, values = lax.while_loop(lambda s: (s[0] < rounds)[0], again, (turn + 1, values))

    posterior = pl.pallas_call(
        functools.partial(sweep_kernel, members),
        out_shape=jax.ShapeDtypeStruct((stack, members, columns), F32),
        in_specs=[smem] * 3 + [vmem] * 8 + [hbm] * 2,
        out_specs=hbm,
        scratch_shapes=[
            pltpu.VMEM((stack, members, columns), F32),
            pltpu.VMEM((stack, DEPTH, columns), BF16),
            pltpu.VMEM((LANES, total), F32),
            pltpu.VMEM((batches, members, obs), F32),
            pltpu.VMEM((batches, DEPTH, obs), BF16),
            pltpu.VMEM((batches, 3 * obs, DEPTH), BF16),
            pltpu.VMEM((GROUP * members, DEPTH), F32),
            pltpu.VMEM((GROUP * members, DEPTH), BF16),
            pltpu.SemaphoreType.DMA((3 * columns // CHUNK,)),
        ],
        compiler_params=pltpu.CompilerParams(vmem_limit_bytes=60 * 1024 * 1024),
        name="sweep",
    )(
        bounds,
        segments,
        tile_order,
        obs_values,
        window_start,
        window_span,
        gain_mean,
        gain_spread,
        ocean_mask.reshape(1, -1),
        reach,
        values,
        parts,
        by_stack,
    )
    return posterior.transpose(1, 0, 2)


def solution(mesh):
    split = Mesh(mesh.devices.reshape(mesh.shape["row"], 4, 4, 2), ROW_COL)
    in_specs = (P(None, None, ROW_COL), P(ROW_COL), P(), P(), P(), P(), P(), P(), P(), P())
    return jax.shard_map(
        per_device, mesh=split, in_specs=in_specs, out_specs=P(None, None, ROW_COL), check_vma=False
    )
```
